32 devices in a mesh: cuts: 4 (over y, x), gz: 8 (over z, core).
Axes of the slice: x: 2, y: 2, z: 4, core: 2. Of those that a mesh axis runs over, the one named last changes fastest.
Arguments:
- vectors: float32 [4, 32, 16, 128, 128], P('cuts', None, 'gz'), may hold values from -9 to 9
- onsite: float32 [16, 128, 128], P('gz'), may hold values from -8.25 to 8.25
- center: float32 [4], P('cuts'), may hold values from -3 to 3
- inv_half: float32 [4], P('cuts'), may hold values from 0.06 to 0.1
- cheb_coef: float32 [4, 3], P('cuts'), may hold values from 0.5 to 1.5
Outputs:
- basis: float32 [4, 64, 16, 128, 128], P('cuts', None, 'gz')
- projected: float32 [4, 64, 64], P('cuts')
The draws below stay inside these ranges and needn't reach their ends.
All inputs are finite; a program needn't handle non-finite values.
Results may differ from the reference program's by a relative error of at most 0.00018.
Values sent between devices are 32-bit elements; how exact they have to be, the bound alone decides.
No kernel may reach another device: no remote copies, remote signals or barrier semaphores. Data moves between devices by JAX's collectives and lax.ppermute only.
A program may use at most 128 MiB of HBM per device.

```python
import jax
import jax.numpy as jnp
from jax import lax

K = 32
LX = 128
LY = 128
NZ = 16
N_CUTS = 4


def draw_vectors(key, part):
    key_shared = jax.random.fold_in(key, 11)
    key_own = jax.random.fold_in(key, 12)
    key_common = jax.random.fold_in(key, 13)
    shared = jnp.clip(jax.random.normal(key_shared, (1, K, NZ, LX, LY), jnp.float32), -6.0, 6.0)
    own = jnp.clip(jax.random.normal(key_own, (N_CUTS, K, NZ, LX, LY), jnp.float32), -6.0, 6.0)
    common = jnp.clip(jax.random.normal(key_common, (1, 1, NZ, LX, LY), jnp.float32), -6.0, 6.0)
    return 0.6 * shared + 0.5 * own + 0.4 * common


def levels(stream_key, extent, cuts, low, top_value):
    factor_of = 1.0
    for axis_at, parts in cuts:
        heights = jax.random.uniform(jax.random.fold_in(jax.random.fold_in(stream_key, 6), axis_at), (parts,), jnp.float32, low / len(cuts), top_value / len(cuts))
        factor_of = factor_of * jnp.repeat(jnp.exp(heights), extent[axis_at] // parts).reshape((-1,) + (1,) * (len(extent) - 1 - axis_at))
    return factor_of


def setup_inputs(seed: int = 0) -> dict:
    splits = jax.random.split(jax.random.key(seed), 6)
    return {
        "vectors": draw_vectors(jax.random.fold_in(splits[5], 71), 0),
        "onsite": jnp.clip(jax.random.uniform(splits[1], (NZ, LX, LY), jnp.float32, -8.25, 8.25) * levels(splits[1], (NZ, LX, LY), ((0, 8),), -0.4, 0.0), -8.25, 8.25),
        "center": jnp.clip(jax.random.uniform(splits[2], (N_CUTS,), jnp.float32, -3.0, 3.0) * levels(splits[2], (N_CUTS,), ((0, 4),), -0.4, 0.0), -3.0, 3.0),
        "inv_half": jnp.clip(0.06 + 0.040000003 * jax.random.uniform(splits[3], (N_CUTS,), jnp.float32) ** levels(splits[3], (N_CUTS,), ((0, 4),), -0.2, 0.2), 0.06, 0.1),
        "cheb_coef": jnp.clip(0.5 + 1.0 * jax.random.uniform(splits[4], (N_CUTS, 3), jnp.float32) ** levels(splits[4], (N_CUTS, 3), ((0, 4),), -0.2, 0.2), 0.5, 1.5),
    }


def neighbours_xy(middle):
    padded = jnp.pad(middle, ((0, 0), (0, 0), (1, 1), (1, 1)))
    return padded[:, :, 2:, 1:-1] + padded[:, :, :-2, 1:-1] + padded[:, :, 1:-1, 2:] + padded[:, :, 1:-1, :-2]

def hamiltonian(field, onsite):
    along_z = jnp.roll(field, 1, axis=1) + jnp.roll(field, -1, axis=1)
    return onsite[None] * field - along_z - neighbours_xy(field)

def reference(vectors, onsite, center, inv_half, cheb_coef):
    sites_all = NZ * LX * LY
    identity = jnp.eye(2 * K, dtype=jnp.float32)
    filtered = []
    for cut_index in range(N_CUTS):
        start = vectors[cut_index]
        first = inv_half[cut_index] * (hamiltonian(start, onsite) - center[cut_index] * start)
        second = 2.0 * inv_half[cut_index] * (hamiltonian(first, onsite) - center[cut_index] * first) - start
        filtered.append(cheb_coef[cut_index, 0] * start + cheb_coef[cut_index, 1] * first + cheb_coef[cut_index, 2] * second)
    bases = []
    projections = []
    for cut_index in range(N_CUTS):
        if cut_index + 1 < N_CUTS:
            partner = filtered[cut_index + 1]
        else:
            partner = jnp.zeros_like(filtered[cut_index])
        union = jnp.concatenate([filtered[cut_index], partner], 0).reshape(2 * K, -1)
        gram = jnp.dot(union.astype(jnp.float32), union.T.astype(jnp.float32), precision=lax.Precision.HIGHEST, preferred_element_type=jnp.float32) / sites_all + 0.25 * identity
        factor = jnp.linalg.cholesky(gram)
        inverse = jax.scipy.linalg.solve_triangular(factor, identity, lower=True)
        basis = jnp.dot(inverse.astype(jnp.float32), union.astype(jnp.float32), precision=lax.Precision.HIGHEST, preferred_element_type=jnp.float32)
        images = hamiltonian(basis.reshape(2 * K, NZ, LX, LY), onsite).reshape(2 * K, -1)
        projections.append(jnp.dot(basis.astype(jnp.float32), images.T.astype(jnp.float32), precision=lax.Precision.HIGHEST, preferred_element_type=jnp.float32) / sites_all)
        bases.append(basis.reshape(2 * K, NZ, LX, LY))
    return (jnp.stack(bases), jnp.stack(projections))
```

```python
import functools

import jax
import jax.numpy as jnp
from jax import lax
from jax.experimental import pallas as pl
from jax.experimental.pallas import tpu as pltpu
from jax.sharding import PartitionSpec as P

F32 = jnp.float32
GROUP = 8
ROWS = 8
VMEM = pl.BlockSpec(memory_space=pltpu.VMEM)
SMEM = pl.BlockSpec(memory_space=pltpu.SMEM)
PARAMS = pltpu.CompilerParams(vmem_limit_bytes=48 * 1024 * 1024)


def dot_nt(left, right):
    return lax.dot_general(
        left, right, (((1,), (1,)), ((), ())), precision=lax.Precision.HIGHEST, preferred_element_type=F32
    )


def dot_nn(left, right):
    return jnp.dot(left, right, precision=lax.Precision.HIGHEST, preferred_element_type=F32)


def struct(*shape):
    return jax.ShapeDtypeStruct(shape, F32)


def cost(flops, nbytes):
    return pl.CostEstimate(flops=int(flops), bytes_accessed=int(nbytes), transcendentals=0)


def chunk_kernel(odd_ref, v_ref, out_ref):
    rows = v_ref.shape[2]
    flat = v_ref.reshape(GROUP * rows, v_ref.shape[3])
    for j in range(rows):
        out_ref[0, j] = flat[pl.ds(j, GROUP, stride=rows), :]


def to_chunk(field, odd, which):
    _, layers, size_x, size_y = field.shape
    rows = 32
    return pl.pallas_call(
        chunk_kernel,
        grid_spec=pltpu.PrefetchScalarGridSpec(
            num_scalar_prefetch=1,
            grid=(layers, size_x // rows),
            in_specs=[
                pl.BlockSpec((GROUP, 1, rows, size_y), lambda s, b, odd: (which, (s + odd[0]) % 2, b, 0))
            ],
            out_specs=pl.BlockSpec((1, rows, GROUP, size_y), lambda s, b, odd: (s, b, 0, 0)),
        ),
        out_shape=struct(layers, size_x, GROUP, size_y),
        compiler_params=PARAMS,
        name="to_chunk",
    )(odd, field)


def beside_in_y(value):
    lane = lax.broadcasted_iota(jnp.int32, value.shape, 1)
    size = value.shape[1]
    left = jnp.where(lane > 0, pltpu.roll(value, 1, 1), 0.0)
    right = jnp.where(lane < size - 1, pltpu.roll(value, size - 1, 1), 0.0)
    return left + right


def filter_kernel(odd_ref, coef_ref, own, inter, intra, ons, ons_inter, ons_intra, out, pay_inter, pay_intra, t1):
    size_x = own.shape[1]
    blocks = size_x // ROWS
    middle, a, b, g = coef_ref[0], coef_ref[1], coef_ref[2], coef_ref[3]
    planes = (inter.at[1], inter.at[0], own.at[0], own.at[1], intra.at[1], intra.at[0])
    sites = (None, ons_inter, ons.at[0], ons.at[1], ons_intra, None)

    def rows_around(ref, block, i):
        x = block * ROWS + i
        low = ref[jnp.maximum(x - 1, 0)] if i == 0 else ref[x - 1]
        high = ref[jnp.minimum(x + 1, size_x - 1)] if i == ROWS - 1 else ref[x + 1]
        if i == 0:
            low = jnp.where(block > 0, low, 0.0)
        if i == ROWS - 1:
            high = jnp.where(block < blocks - 1, high, 0.0)
        return low + high

    def shifted(ref, before, after, site, block, i):
        x = block * ROWS + i
        value = ref[x]
        around = rows_around(ref, block, i) + beside_in_y(value) + (before[x] + after[x])
        return (site[pl.ds(x, 1), :] - middle) * value - around

    def first(block, _):
        for k in range(1, 5):
            for i in range(ROWS):
                t1[k - 1, block * ROWS + i] = shifted(
                    planes[k], planes[k - 1], planes[k + 1], sites[k], block, i
                )
        return 0

    def second(block, _):
        for k in range(2, 4):
            for i in range(ROWS):
                x = block * ROWS + i
                twice = shifted(t1.at[k - 1], t1.at[k - 2], t1.at[k], sites[k], block, i)
                out[k - 2, x] = a * planes[k][x] + b * t1[k - 1, x] + g * twice
        return 0

    lax.fori_loop(0, blocks, first, 0)
    lax.fori_loop(0, blocks, second, 0)
    start = (1 - odd_ref[0]) * (size_x // 2)

    def pay(block, _):
        here = pl.ds(block * ROWS, ROWS)
        there = pl.ds(start + block * ROWS, ROWS)
        pay_inter[here] = out[0, there]
        pay_intra[here] = out[1, there]
        return 0

    lax.fori_loop(0, size_x // 2 // ROWS, pay, 0)


def filter_chunk(odd, coef, own, inter, intra, ons, ons_inter, ons_intra):
    _, size_x, _, size_y = own.shape
    half = struct(size_x // 2, GROUP, size_y)
    return pl.pallas_call(
        filter_kernel,
        in_specs=[SMEM, SMEM] + [VMEM] * 6,
        out_specs=[VMEM] * 3,
        out_shape=[struct(*own.shape), half, half],
        scratch_shapes=[pltpu.VMEM((4, size_x, GROUP, size_y), F32)],
        compiler_params=PARAMS,
        cost_estimate=cost(60 * own.size, 20 * own.size),
        name="filter_chunk",
    )(odd, coef, own, inter, intra, ons, ons_inter, ons_intra)


def wide(refs, side, x, rows):
    return jnp.concatenate(
        [jnp.concatenate([ref[side, x + i] for i in range(rows)], axis=1) for ref in refs], axis=0
    )


def image_rows(refs, ons, side, block, rows):
    size_x, size_y = refs[0].shape[1], refs[0].shape[3]
    blocks = size_x // rows
    lane = lax.broadcasted_iota(jnp.int32, (GROUP, size_y), 1)
    groups = []
    for ref in refs:
        pieces = []
        for i in range(rows):
            x = block * rows + i
            value = ref[side, x]
            if i < rows - 1:
                after = ref[side, x + 1]
            else:
                after = jnp.where(block < blocks - 1, ref[side, jnp.minimum(x + 1, size_x - 1)], 0.0)
            after = after + jnp.where(lane < size_y - 1, pltpu.roll(value, size_y - 1, 1), 0.0)
            if side == 0:
                after = after + ref[1, x]
            pieces.append(ons[side, pl.ds(x, 1), :] * value - 2.0 * after)
        groups.append(jnp.concatenate(pieces, axis=1))
    return jnp.concatenate(groups, axis=0)


def own_kernel(count, *refs):
    own, ons, gram, energy = refs[:count], refs[count], refs[count + 1], refs[count + 2]
    size_x = own[0].shape[1]

    def step(block, totals):
        for side in range(2):
            left = wide(own, side, block * ROWS, ROWS)
            right = jnp.concatenate([left, image_rows(own, ons, side, block, ROWS)], axis=0)
            totals = totals + dot_nt(left, right)
        return totals

    size = count * GROUP
    total = lax.fori_loop(0, size_x // ROWS, step, jnp.zeros((size, 2 * size), F32))
    gram[...] = total[:, :size]
    energy[...] = total[:, size:]


def own_products(own, ons):
    size = len(own) * GROUP
    return pl.pallas_call(
        functools.partial(own_kernel, len(own)),
        in_specs=[VMEM] * (len(own) + 1),
        out_specs=[VMEM] * 2,
        out_shape=[struct(size, size)] * 2,
        compiler_params=PARAMS,
        cost_estimate=cost(24 * size * len(own) * own[0].size, 4 * len(own) * own[0].size),
        name="own_products",
    )(*own, ons)


def cross_gram_kernel(count, *refs):
    own, other, gram = refs[:count], refs[count : 2 * count], refs[2 * count]
    size_x = own[0].shape[1]

    def step(block, total):
        for side in range(2):
            total = total + dot_nt(wide(other, side, block * ROWS, ROWS), wide(own, side, block * ROWS, ROWS))
        return total

    size = count * GROUP
    gram[...] = lax.fori_loop(0, size_x // ROWS, step, jnp.zeros((size, size), F32))


def cross_gram(own, other):
    size = len(own) * GROUP
    return pl.pallas_call(
        functools.partial(cross_gram_kernel, len(own)),
        in_specs=[VMEM] * (2 * len(own)),
        out_specs=VMEM,
        out_shape=struct(size, size),
        compiler_params=PARAMS,
        cost_estimate=cost(12 * size * len(own) * own[0].size, 8 * len(own) * own[0].size),
        name="cross_gram",
    )(*own, *other)


def cross_energy_kernel(count, *refs):
    own, other, ons, energy = refs[:count], refs[count : 2 * count], refs[2 * count], refs[2 * count + 1]
    size_x = own[0].shape[1]

    def step(block, total):
        for side in range(2):
            total = total + dot_nt(wide(other, side, block * ROWS, ROWS), image_rows(own, ons, side, block, ROWS))
            total = total + dot_nt(image_rows(other, ons, side, block, ROWS), wide(own, side, block * ROWS, ROWS))
        return total

    size = count * GROUP
    energy[...] = lax.fori_loop(0, size_x // ROWS, step, jnp.zeros((size, size), F32))


def cross_energy(own, other, ons):
    size = len(own) * GROUP
    return pl.pallas_call(
        functools.partial(cross_energy_kernel, len(own)),
        in_specs=[VMEM] * (2 * len(own) + 1),
        out_specs=VMEM,
        out_shape=struct(size, size),
        compiler_params=PARAMS,
        cost_estimate=cost(24 * size * len(own) * own[0].size, 8 * len(own) * own[0].size),
        name="cross_energy",
    )(*own, *other, ons)


def border_kernel(count, odd_ref, *refs):
    own, other, inter, intra, other_inter, other_intra = (refs[count * i : count * (i + 1)] for i in range(6))
    energy, cross, out = refs[6 * count :]
    half = inter[0].shape[0]
    start = odd_ref[0] * half

    def halo(parts, x):
        return jnp.concatenate(
            [jnp.concatenate([ref[x + i] for i in range(ROWS)], axis=1) for ref in parts], axis=0
        )

    def step(block, totals):
        one, two = totals
        x = block * ROWS
        for side, mine, theirs in ((0, inter, other_inter), (1, intra, other_intra)):
            here = wide(own, side, start + x, ROWS)
            both = jnp.concatenate([here, wide(other, side, start + x, ROWS)], axis=0)
            one = one + dot_nt(both, halo(mine, x))
            two = two + dot_nt(halo(theirs, x), here)
        return one, two

    size = count * GROUP
    zeros = jnp.zeros((2 * size, size), F32), jnp.zeros((size, size), F32)
    one, two = lax.fori_loop(0, half // ROWS, step, zeros)
    out[:size] = energy[...] - 2.0 * one[:size]
    out[size:] = cross[...] - 2.0 * (one[size:] + two)


def border_energy(odd, own, other, inter, intra, other_inter, other_intra, energy, cross):
    count = len(own)
    size = count * GROUP
    return pl.pallas_call(
        functools.partial(border_kernel, count),
        in_specs=[SMEM] + [VMEM] * (6 * count + 2),
        out_specs=VMEM,
        out_shape=struct(2 * size, size),
        compiler_params=PARAMS,
        cost_estimate=cost(18 * size * count * own[0].size, 12 * count * own[0].size),
        name="border_energy",
    )(odd, *own, *other, *inter, *intra, *other_inter, *other_intra, energy, cross)


def inverse_factor(matrix):
    size = matrix.shape[0]
    row = lax.broadcasted_iota(jnp.int32, (size, size), 0)
    col = lax.broadcasted_iota(jnp.int32, (size, size), 1)
    work = jnp.concatenate([matrix, jnp.where(row == col, 1.0, 0.0)], axis=1)
    below = lax.broadcasted_iota(jnp.int32, work.shape, 0)
    for j in range(size):
        pivot = work[j : j + 1, :]
        scale = 1.0 / jnp.sqrt(pivot[:, j : j + 1])
        pivot = pivot * scale
        ratio = work[:, j : j + 1] * scale
        work = jnp.where(below > j, work - ratio * pivot, jnp.where(below == j, pivot, work))
    return work[:, size:]


def with_shift(gram, scale):
    row = lax.broadcasted_iota(jnp.int32, gram.shape, 0)
    col = lax.broadcasted_iota(jnp.int32, gram.shape, 1)
    return gram * scale + jnp.where(row == col, 0.25, 0.0)


def top_kernel(scale, gram, out):
    out[...] = inverse_factor(with_shift(gram[...], scale))


def top_factor(gram, scale):
    return pl.pallas_call(
        functools.partial(top_kernel, scale),
        in_specs=[VMEM],
        out_specs=VMEM,
        out_shape=struct(*gram.shape),
        compiler_params=PARAMS,
        name="top_factor",
    )(gram)


def bottom_kernel(scale, cross, gram, top, out):
    low = dot_nt(cross[...] * scale, top[...])
    inverse = inverse_factor(with_shift(gram[...], scale) - dot_nt(low, low))
    out[:, : low.shape[0]] = -dot_nn(inverse, dot_nn(low, top[...]))
    out[:, low.shape[0] :] = inverse


def bottom_factor(cross, gram, top, scale):
    size = gram.shape[0]
    return pl.pallas_call(
        functools.partial(bottom_kernel, scale),
        in_specs=[VMEM] * 3,
        out_specs=VMEM,
        out_shape=struct(size, 2 * size),
        compiler_params=PARAMS,
        name="bottom_factor",
    )(cross, gram, top)


def basis_kernel(count, odd_ref, *refs):
    parts, coef, out = refs[:count], refs[count], refs[-1]
    rows = parts[0].shape[1]
    result = dot_nn(coef[...], wide(parts, 0, 0, rows))
    flat = out.reshape(out.shape[0] * rows, out.shape[3])
    for i in range(rows):
        size = parts[0].shape[3]
        flat[pl.ds(i, out.shape[0], stride=rows), :] = result[:, i * size : (i + 1) * size]


def basis_half(odd, parts, coef, which, into):
    layers, size_x, _, size_y = parts[0].shape
    size = coef.shape[0]
    rows = 16
    part = pl.BlockSpec((1, rows, GROUP, size_y), lambda s, b, odd: (s, b, 0, 0))
    matrix = pl.BlockSpec(coef.shape, lambda s, b, odd: (0, 0))
    operands = [odd, *parts, coef]
    in_specs = [part] * len(parts) + [matrix]
    aliases = {}
    if into is not None:
        aliases = {len(operands): 0}
        operands.append(into)
        in_specs.append(pl.BlockSpec(memory_space=pl.ANY))
    return pl.pallas_call(
        functools.partial(basis_kernel, len(parts)),
        grid_spec=pltpu.PrefetchScalarGridSpec(
            num_scalar_prefetch=1,
            grid=(layers, size_x // rows),
            in_specs=in_specs,
            out_specs=pl.BlockSpec(
                (size, 1, rows, size_y), lambda s, b, odd: (which, (s + odd[0]) % 2, b, 0)
            ),
        ),
        out_shape=struct(2 * size, layers, size_x, size_y),
        input_output_aliases=aliases,
        compiler_params=PARAMS,
        cost_estimate=cost(12 * size * len(parts) * parts[0].size, 8 * len(parts) * parts[0].size),
        name="basis_half",
    )(*operands)


def project_kernel(scale, energy, other, top, bottom, out):
    size = top.shape[0]
    here, there = energy[:size], other[...]
    cross = energy[size:]
    upper = jnp.concatenate([here + here.T, cross.T], axis=1)
    lower = jnp.concatenate([cross, there + there.T], axis=1)
    matrix = jnp.concatenate([upper, lower], axis=0) * (0.5 * scale)
    inverse = jnp.concatenate(
        [jnp.concatenate([top[...], jnp.zeros_like(top)], axis=1), bottom[...]], axis=0
    )
    out[...] = dot_nt(dot_nn(inverse, matrix), inverse)


def project(energy, other, top, bottom, scale):
    size = top.shape[0]
    return pl.pallas_call(
        functools.partial(project_kernel, scale),
        in_specs=[VMEM] * 4,
        out_specs=VMEM,
        out_shape=struct(2 * size, 2 * size),
        compiler_params=PARAMS,
        name="project",
    )(energy, other, top, bottom)


def sum_over(value, axis):
    size = lax.axis_size(axis)
    if size & (size - 1):
        return lax.psum(value, axis)
    step = 1
    while step < size:
        value = value + lax.ppermute(value, axis, [(i, i ^ step) for i in range(size)])
        step *= 2
    return value


def body(vectors, onsite, center, inv_half, cheb_coef):
    field = vectors[0]
    count, layers, size_x, size_y = field.shape
    ring = lax.axis_size("gz")
    cuts = lax.axis_size("cuts")
    scale = 1.0 / (layers * ring * size_x * size_y)
    odd = (lax.axis_index("gz") % 2).astype(jnp.int32)[None]
    across = [(i, (i + 1) % ring if i % 2 else (i - 1) % ring) for i in range(ring)]
    pair = [(i, i ^ 1) for i in range(ring)]
    left = [(i, i - 1) for i in range(1, cuts)]

    def inter_swap(value):
        return lax.ppermute(value, "gz", across)

    def intra_swap(value):
        return lax.ppermute(value, "gz", pair)

    def from_next(value):
        return lax.ppermute(value, "cuts", left)

    h, c0, c1, c2 = inv_half[0], cheb_coef[0, 0], cheb_coef[0, 1], cheb_coef[0, 2]
    coef = jnp.stack([center[0], c0 - c2, c1 * h, 2.0 * c2 * h * h])
    ons = jnp.where(odd[0] == 0, onsite, onsite[::-1])
    groups = range(count // GROUP)

    mine = [to_chunk(field, odd, i) for i in groups]
    far = [inter_swap(m) for m in mine]
    near = [intra_swap(m) for m in mine]
    ons_far, ons_near = inter_swap(ons[0]), intra_swap(ons[1])
    own, other, edge_far, edge_near = [], [], [], []
    for i in groups:
        filtered, pay_far, pay_near = filter_chunk(odd, coef, mine[i], far[i], near[i], ons, ons_far, ons_near)
        own.append(filtered)
        other.append(from_next(filtered))
        edge_far.append(inter_swap(pay_far))
        edge_near.append(intra_swap(pay_near))
    start = (1 - odd[0]) * (size_x // 2)
    other_far = [from_next(e) for e in edge_far]
    other_near = [intra_swap(lax.dynamic_slice_in_dim(o[1], start, size_x // 2, 0)) for o in other]

    gram, energy = own_products(own, ons)
    gram = sum_over(gram, "gz")
    gram_next = from_next(gram)
    top = top_factor(gram, scale)
    basis = basis_half(odd, own, top, 0, None)
    cross = sum_over(cross_gram(own, other), "gz")
    bottom = bottom_factor(cross, gram_next, top, scale)
    basis = basis_half(odd, own + other, bottom, 1, basis)

    mixed = cross_energy(own, other, ons)
    total = border_energy(odd, own, other, edge_far, edge_near, other_far, other_near, energy, mixed)
    total = sum_over(total, "gz")
    total_next = from_next(total[: count])
    projected = project(total, total_next, top, bottom, scale)
    return basis[None], projected[None]


def solution(mesh):
    in_specs = (
        P("cuts", None, "gz", None, None),
        P("gz", None, None),
        P("cuts"),
        P("cuts"),
        P("cuts", None),
    )
    out_specs = (P("cuts", None, "gz", None, None), P("cuts", None, None))
    return jax.shard_map(body, mesh=mesh, in_specs=in_specs, out_specs=out_specs, check_vma=False)
```

```python
import functools

import jax
import jax.numpy as jnp
from jax import lax
from jax.experimental import pallas as pl
from jax.experimental.pallas import tpu as pltpu
from jax.sharding import PartitionSpec as P

F32 = jnp.float32
GROUP = 8
ROWS = 8
SPAN = 64
VMEM = pl.BlockSpec(memory_space=pltpu.VMEM)
SMEM = pl.BlockSpec(memory_space=pltpu.SMEM)
PARAMS = pltpu.CompilerParams(vmem_limit_bytes=24 * 1024 * 1024)

TERMS = ((2, 0), (1, 1), (0, 2), (1, 0), (0, 1), (0, 0))


def three_parts(value):
    parts = []
    for _ in range(3):
        parts.append(value.astype(jnp.bfloat16))
        value = value - parts[-1].astype(F32)
    return jnp.concatenate(parts, axis=0)


def dot_wide(left, right):
    m, n = left.shape[0], right.shape[0]
    terms = lax.dot_general(
        three_parts(left), three_parts(right), (((1,), (1,)), ((), ())), preferred_element_type=F32
    )
    return sum(terms[i * m : (i + 1) * m, j * n : (j + 1) * n] for i, j in TERMS)


def dot_nt(left, right):
    return lax.dot_general(
        left, right, (((1,), (1,)), ((), ())), precision=lax.Precision.HIGHEST, preferred_element_type=F32
    )


def dot_nn(left, right):
    return jnp.dot(left, right, precision=lax.Precision.HIGHEST, preferred_element_type=F32)


def struct(*shape):
    return jax.ShapeDtypeStruct(shape, F32)


def cost(flops, nbytes):
    return pl.CostEstimate(flops=int(flops), bytes_accessed=int(nbytes), transcendentals=0)


SMALL = cost(1000, 1000)


def chunk_kernel(odd_ref, field0, field1, onsite_ref, out):
    size_x = field0.shape[2]
    for layer, source in enumerate((field0, field1)):
        flat = source.reshape(GROUP * size_x, source.shape[3])
        for j in range(size_x):
            out[layer * size_x + j] = flat[pl.ds(j, GROUP, stride=size_x), :]
    for j in range(out.shape[0] - 2 * size_x):
        out[2 * size_x + j] = onsite_ref[0, j * GROUP : (j + 1) * GROUP, :]


def to_chunk(field, onsite, odd, which):
    _, layers, size_x, size_y = field.shape
    rows = layers * size_x + (size_x // GROUP if which == 0 else 0)
    return pl.pallas_call(
        chunk_kernel,
        grid_spec=pltpu.PrefetchScalarGridSpec(
            num_scalar_prefetch=1,
            grid=(1,),
            in_specs=[
                pl.BlockSpec((GROUP, 1, size_x, size_y), lambda b, odd: (which, odd[0], 0, 0)),
                pl.BlockSpec((GROUP, 1, size_x, size_y), lambda b, odd: (which, 1 - odd[0], 0, 0)),
                pl.BlockSpec((1, size_x, size_y), lambda b, odd: (odd[0], 0, 0)),
            ],
            out_specs=pl.BlockSpec((rows, GROUP, size_y), lambda b, odd: (0, 0, 0)),
        ),
        out_shape=struct(rows, GROUP, size_y),
        compiler_params=PARAMS,
        cost_estimate=SMALL,
        name="to_chunk",
    )(odd, field, field, onsite)


def beside_in_y(value):
    lane = lax.broadcasted_iota(jnp.int32, value.shape, 1)
    size = value.shape[1]
    left = jnp.where(lane > 0, pltpu.roll(value, 1, 1), 0.0)
    right = jnp.where(lane < size - 1, pltpu.roll(value, size - 1, 1), 0.0)
    return left + right


def beside(ref, x, first, last):
    size_x = ref.shape[0]
    low = ref[x - 1] if first is None else jnp.where(first, ref[jnp.maximum(x - 1, 0)], 0.0)
    high = ref[x + 1] if last is None else jnp.where(last, ref[jnp.minimum(x + 1, size_x - 1)], 0.0)
    return (low + high) + beside_in_y(ref[x])


def over_rows(size_x, step):
    blocks = size_x // ROWS

    def wrapped(block, _):
        for i in range(ROWS):
            first = block > 0 if i == 0 else None
            last = block < blocks - 1 if i == ROWS - 1 else None
            step(block * ROWS + i, first, last)
        return 0

    lax.fori_loop(0, blocks, wrapped, 0)


def layers_of(ref, size_x):
    return ref.at[pl.ds(0, size_x)], ref.at[pl.ds(size_x, size_x)]


def row_of(site, x):
    return site[pl.ds(x, 1), :]


def factors(center, inv_half, cheb):
    h = inv_half[0]
    return center[0], cheb[0, 0] - cheb[0, 2], cheb[0, 1] * h, 2.0 * cheb[0, 2] * h * h


def local_kernel(token, center, inv_half, cheb, own, near, ons, ons_near, out, once, inner):
    size_x = once.shape[0]
    middle, a, b, g = factors(center, inv_half, cheb)
    own0, own1 = layers_of(own, size_x)
    near0, near1 = layers_of(near, size_x)
    out0, out1 = layers_of(out, size_x)

    def layer(here, sides, beyond, site, side_sites, result):
        def first(x, top, end):
            around = sum(side[x] for side in sides)
            t = (row_of(site, x) - middle) * here[x] - beside(here, x, top, end) - around
            once[x] = t
            inner[x] = t - around

        def second(x, top, end):
            t = once[x]
            twice = (row_of(site, x) - middle) * t - beside(inner, x, top, end)
            for side, energies in zip(sides, side_sites):
                twice = twice - (row_of(energies, x) - middle) * side[x]
            twice = twice + 2.0 * here[x] + beyond[x]
            result[x] = a * here[x] + b * t + g * twice

        over_rows(size_x, first)
        over_rows(size_x, second)

    layer(own1, (own0, near1), near0, ons.at[1], (ons.at[0], ons_near), out1)
    layer(own0, (own1,), near1, ons.at[0], (ons.at[1],), out0)


def filter_local(token, scalars, own, near, ons, ons_near):
    _, size_x, size_y = ons.shape
    layer = pltpu.VMEM((size_x, GROUP, size_y), F32)
    return pl.pallas_call(
        local_kernel,
        in_specs=[SMEM] * 4 + [VMEM] * 4,
        out_specs=VMEM,
        out_shape=struct(2 * size_x, GROUP, size_y),
        scratch_shapes=[layer, layer],
        compiler_params=PARAMS,
        cost_estimate=SMALL,
        name="filter_local",
    )(token, *scalars, own, near, ons, ons_near)


def far_kernel(odd_ref, center, inv_half, cheb, base, far, ons, ons_far, out, pay):
    _, size_x, size_y = ons.shape
    middle, a, b, g = factors(center, inv_half, cheb)
    base0, base1 = layers_of(base, size_x)
    far0, far1 = layers_of(far, size_x)
    out0, out1 = layers_of(out, size_x)
    shift = b - 2.0 * g * middle

    def step(x, top, end):
        value = far0[x]
        site = g * (row_of(ons.at[0], x) + row_of(ons_far, x)) + shift
        out0[x] = base0[x] + ((2.0 * g) * beside(far0, x, top, end) - site * value + g * far1[x])
        out1[x] = base1[x] + g * value

    over_rows(size_x, step)
    half = size_x // 2
    start = (1 - odd_ref[0]) * half

    def copy(block, _):
        pay[pl.ds(block * ROWS, ROWS)] = out[pl.ds(start + block * ROWS, ROWS)]
        return 0

    lax.fori_loop(0, half // ROWS, copy, 0)


def filter_far(odd, scalars, base, far, ons, ons_far):
    _, size_x, size_y = ons.shape
    return pl.pallas_call(
        far_kernel,
        in_specs=[SMEM] * 4 + [VMEM] * 4,
        out_specs=[VMEM] * 2,
        out_shape=[struct(2 * size_x, GROUP, size_y), struct(size_x // 2, GROUP, size_y)],
        compiler_params=PARAMS,
        cost_estimate=SMALL,
        name="filter_far",
    )(odd, *scalars, base, far, ons, ons_far)


def image_kernel(token, own, beyond, ons, out):
    size_x = ons.shape[1]
    own0, own1 = layers_of(own, size_x)
    out0, out1 = layers_of(out, size_x)

    def step(x, top, end):
        value0, value1 = own0[x], own1[x]
        out0[x] = row_of(ons.at[0], x) * value0 - beside(own0, x, top, end) - value1
        out1[x] = row_of(ons.at[1], x) * value1 - beside(own1, x, top, end) - (value0 + beyond[size_x + x])

    over_rows(size_x, step)


def stage_kernel(token, center, inv_half, cheb, own, beyond, mine, near, ons, ons_near, image, base, once, inner):
    image_kernel(token, own, beyond, ons, image)
    local_kernel(token, center, inv_half, cheb, mine, near, ons, ons_near, base, once, inner)


def stage(token, scalars, own, beyond, mine, near, ons, ons_near):
    _, size_x, size_y = ons.shape
    layer = pltpu.VMEM((size_x, GROUP, size_y), F32)
    chunk = struct(2 * size_x, GROUP, size_y)
    return pl.pallas_call(
        stage_kernel,
        in_specs=[SMEM] * 4 + [VMEM] * 6,
        out_specs=[VMEM] * 2,
        out_shape=[chunk, chunk],
        scratch_shapes=[layer, layer],
        compiler_params=PARAMS,
        cost_estimate=SMALL,
        name="stage",
    )(token, *scalars, own, beyond, mine, near, ons, ons_near)


def image_chunk(token, own, beyond, ons):
    return pl.pallas_call(
        image_kernel,
        in_specs=[SMEM] + [VMEM] * 3,
        out_specs=VMEM,
        out_shape=struct(*own.shape),
        compiler_params=PARAMS,
        cost_estimate=SMALL,
        name="image_chunk",
    )(token, own, beyond, ons)


def wide(refs, x, rows):
    return jnp.concatenate([jnp.concatenate([ref[x + i] for i in range(rows)], axis=1) for ref in refs], axis=0)


def products_kernel(lefts, token, *refs):
    left, right, out = refs[:lefts], refs[lefts:-1], refs[-1]
    rows = left[0].shape[0]

    @pl.when(pl.program_id(0) == 0)
    def _():
        out[...] = jnp.zeros_like(out)

    here = wide(left, 0, rows)
    there = jnp.concatenate([here, wide(right, 0, rows)], axis=0)
    out[...] += dot_wide(here, there)


def products(token, left, right):
    rows_all, _, size_y = left[0].shape
    part = pl.BlockSpec((SPAN, GROUP, size_y), lambda b, token: (b, 0, 0))
    shape = (len(left) * GROUP, (len(left) + len(right)) * GROUP)
    return pl.pallas_call(
        functools.partial(products_kernel, len(left)),
        grid_spec=pltpu.PrefetchScalarGridSpec(
            num_scalar_prefetch=1,
            grid=(rows_all // SPAN,),
            in_specs=[part] * (len(left) + len(right)),
            out_specs=pl.BlockSpec(shape, lambda b, token: (0, 0)),
        ),
        out_shape=struct(*shape),
        compiler_params=PARAMS,
        cost_estimate=SMALL,
        name="products",
    )(token, *left, *right)


def border_kernel(lefts, flip, odd_ref, *refs):
    left, stacks, out = refs[:lefts], refs[lefts:-1], refs[-1]
    right = [stack.at[i] for stack in stacks for i in range(stack.shape[0])]
    half = left[0].shape[0]

    def step(block, total):
        x = block * SPAN
        here, there = wide(left, x, SPAN), wide(right, x, SPAN)
        return total + (dot_wide(there, here) if flip else dot_wide(here, there))

    out[...] = lax.fori_loop(0, half // SPAN, step, jnp.zeros(out.shape, F32))


def border_products(odd, own, halos, flip=False):
    _, half, _, size_y = halos[0].shape
    m, n = len(own) * GROUP, sum(stack.shape[0] for stack in halos) * GROUP
    shape = (n, m) if flip else (m, n)
    mine = pl.BlockSpec((half, GROUP, size_y), lambda b, odd: (odd[0], 0, 0))
    theirs = [pl.BlockSpec(stack.shape, lambda b, odd: (0, 0, 0, 0)) for stack in halos]
    return pl.pallas_call(
        functools.partial(border_kernel, len(own), flip),
        grid_spec=pltpu.PrefetchScalarGridSpec(
            num_scalar_prefetch=1,
            grid=(1,),
            in_specs=[mine] * len(own) + theirs,
            out_specs=pl.BlockSpec(shape, lambda b, odd: (0, 0)),
        ),
        out_shape=struct(*shape),
        compiler_params=PARAMS,
        cost_estimate=SMALL,
        name="border_products",
    )(odd, *own, *halos)


def inverse_factor(matrix):
    size = matrix.shape[0]
    row = lax.broadcasted_iota(jnp.int32, (size, size), 0)
    col = lax.broadcasted_iota(jnp.int32, (size, size), 1)
    work = jnp.concatenate([matrix, jnp.where(row == col, 1.0, 0.0)], axis=1)
    below = lax.broadcasted_iota(jnp.int32, work.shape, 0)
    for j in range(size):
        pivot = work[j : j + 1, :]
        scale = 1.0 / jnp.sqrt(pivot[:, j : j + 1])
        pivot = pivot * scale
        ratio = work[:, j : j + 1] * scale
        work = jnp.where(below > j, work - ratio * pivot, jnp.where(below == j, pivot, work))
    return work[:, size:]


def with_shift(gram, scale):
    row = lax.broadcasted_iota(jnp.int32, gram.shape, 0)
    col = lax.broadcasted_iota(jnp.int32, gram.shape, 1)
    return gram * scale + jnp.where(row == col, 0.25, 0.0)


def top_kernel(scale, gram, out):
    out[...] = inverse_factor(with_shift(gram[...], scale))


def top_factor(gram, scale):
    return pl.pallas_call(
        functools.partial(top_kernel, scale),
        in_specs=[VMEM],
        out_specs=VMEM,
        out_shape=struct(*gram.shape),
        compiler_params=PARAMS,
        name="top_factor",
    )(gram)


def bottom_kernel(scale, grams, top, out):
    size = top.shape[0]
    low = dot_nt(grams[:, size:] * scale, top[...])
    inverse = inverse_factor(with_shift(grams[:, :size], scale) - dot_nt(low, low))
    out[:, :size] = -dot_nn(inverse, dot_nn(low, top[...]))
    out[:, size:] = inverse


def bottom_factor(grams, top, scale):
    size = top.shape[0]
    return pl.pallas_call(
        functools.partial(bottom_kernel, scale),
        in_specs=[VMEM] * 2,
        out_specs=VMEM,
        out_shape=struct(size, 2 * size),
        compiler_params=PARAMS,
        cost_estimate=SMALL,
        name="bottom_factor",
    )(grams, top)


def basis_kernel(count, odd_ref, *refs):
    parts, coef, out = refs[:count], refs[count], refs[-1]
    rows, _, size_y = parts[0].shape
    result = dot_nn(coef[...], wide(parts, 0, rows))
    flat = out.reshape(out.shape[0] * rows, size_y)
    for i in range(rows):
        flat[pl.ds(i, out.shape[0], stride=rows), :] = result[:, i * size_y : (i + 1) * size_y]


def basis_half(odd, parts, coef, which, into):
    rows_all, _, size_y = parts[0].shape
    layers, rows = 2, 64
    size_x = rows_all // layers
    blocks = size_x // rows
    size = coef.shape[0]
    part = pl.BlockSpec((rows, GROUP, size_y), lambda s, b, odd: (s * blocks + b, 0, 0))
    operands = [odd, *parts, coef]
    in_specs = [part] * len(parts) + [pl.BlockSpec(coef.shape, lambda s, b, odd: (0, 0))]
    aliases = {}
    if into is not None:
        aliases = {len(operands): 0}
        operands.append(into)
        in_specs.append(pl.BlockSpec(memory_space=pl.ANY))
    return pl.pallas_call(
        functools.partial(basis_kernel, len(parts)),
        grid_spec=pltpu.PrefetchScalarGridSpec(
            num_scalar_prefetch=1,
            grid=(layers, blocks),
            in_specs=in_specs,
            out_specs=pl.BlockSpec(
                (size, 1, rows, size_y), lambda s, b, odd: (which, (s + odd[0]) % 2, b, 0)
            ),
        ),
        out_shape=struct(2 * size, layers, size_x, size_y),
        input_output_aliases=aliases,
        compiler_params=PARAMS,
        cost_estimate=SMALL,
        name="basis_half",
    )(*operands)


def project_kernel(scale, energy, top, bottom, out):
    size = top.shape[0]
    here, cross, there = energy[:size], energy[size : 2 * size], energy[2 * size :]
    upper = jnp.concatenate([here + here.T, cross.T], axis=1)
    lower = jnp.concatenate([cross, there + there.T], axis=1)
    matrix = jnp.concatenate([upper, lower], axis=0) * (0.5 * scale)
    inverse = jnp.concatenate(
        [jnp.concatenate([top[...], jnp.zeros_like(top)], axis=1), bottom[...]], axis=0
    )
    out[...] = dot_nt(dot_nn(inverse, matrix), inverse)


def project(energy, top, bottom, scale):
    size = top.shape[0]
    return pl.pallas_call(
        functools.partial(project_kernel, scale),
        in_specs=[VMEM] * 3,
        out_specs=VMEM,
        out_shape=struct(2 * size, 2 * size),
        compiler_params=PARAMS,
        name="project",
    )(energy, top, bottom)


def behind(value, *others):
    return lax.optimization_barrier((value, *others))[0]


def partial_sums(value, axis, *others):
    size = lax.axis_size(axis)
    if size & (size - 1):
        return [lax.psum(value, axis)]
    sums = []
    step = 1
    while step < size:
        value = value + lax.ppermute(value, axis, [(i, i ^ step) for i in range(size)])
        if step == 1:
            value = behind(value, *others)
        sums.append(value)
        step *= 2
    return sums


def body(vectors, onsite, center, inv_half, cheb_coef):
    field = vectors[0]
    count, layers, size_x, size_y = field.shape
    ring = lax.axis_size("gz")
    cuts = lax.axis_size("cuts")
    scale = 1.0 / (layers * ring * size_x * size_y)
    odd = (lax.axis_index("gz") % 2).astype(jnp.int32)[None]
    across = [(i, (i + 1) % ring if i % 2 else (i - 1) % ring) for i in range(ring)]
    pair = [(i, i ^ 1) for i in range(ring)]
    left = [(i, i - 1) for i in range(1, cuts)]

    def inter_swap(value):
        return lax.ppermute(value, "gz", across)

    def intra_swap(value):
        return lax.ppermute(value, "gz", pair)

    def from_next(value):
        return lax.ppermute(value, "cuts", left)

    scalars = (center, inv_half, cheb_coef)
    ons = jnp.where(odd[0] == 0, onsite, onsite[::-1])
    groups = range(count // GROUP)

    mine, near, far = [], [], []
    token = odd
    for i in groups:
        mine.append(to_chunk(field, onsite, behind(odd, token), i))
        token = mine[-1]
    rows = layers * size_x
    near = [intra_swap(mine[0])]
    ons_near = intra_swap(ons[1])
    for i in groups[1:]:
        near.append(intra_swap(behind(mine[i], near[-1])))
    far = [inter_swap(mine[0]), inter_swap(behind(mine[1], near[0]))]

    def local(i, *tokens):
        return filter_local(behind(odd, *tokens), scalars, mine[i], near[i], ons, ons_near)

    base = local(0, mine[-1])
    far[0] = behind(far[0], base)
    ons_far = far[0][rows:].reshape(size_x, size_y)
    own, other, image, pay, beyond = [], [], [], [], []
    last = len(groups) - 1
    for i in groups:
        out, half = filter_far(behind(odd, base), scalars, base, far[i], ons, ons_far)
        own.append(out)
        pay.append(half)
        other.append(from_next(out))
        beyond.append(intra_swap(out))
        if i + 2 <= last:
            far.append(inter_swap(behind(mine[i + 2], far[i])))
        token = behind(odd, out, *other[i - 1 : i]) if i else behind(odd, out)
        if i == 0:
            base = local(1, token)
        elif i < last:
            done, base = stage(token, scalars, own[i - 1], beyond[i - 1], mine[i + 1], near[i + 1], ons, ons_near)
            image.append(done)
        else:
            image.append(image_chunk(token, own[i - 1], beyond[i - 1], ons))
            image.append(image_chunk(behind(odd, image[-1]), own[i], beyond[i], ons))

    middle = (last + 1) // 2
    halo0 = [inter_swap(behind(jnp.stack(pay[:middle]), own[-1])), inter_swap(jnp.stack(pay[middle:]))]
    both = products(behind(odd, halo0[0]), own, image)
    gram, energy = both[:, :count], both[:, count:]
    gram = partial_sums(gram, "gz", halo0[1])[-1]
    top = top_factor(gram, scale)
    raw = products(behind(odd, top), other, own + image)
    start = (1 - odd[0]) * (size_x // 2)
    next_pay = jnp.stack([lax.dynamic_slice_in_dim(behind(value, top), start, size_x // 2, 0) for value in other[middle:]])
    next_halo0 = [from_next(behind(halo0[0], top)), inter_swap(next_pay)]
    border = border_products(behind(odd, raw), own + other, halo0)
    here = energy - 2.0 * border[:count]
    there = from_next(here)
    beyond = border_products(behind(odd, border), own, next_halo0, True)
    total = 2.0 * (raw[:, 2 * count :] - border[count:] - beyond)
    total = jnp.concatenate([raw[:, : 2 * count], jnp.concatenate([here, total], axis=1)], axis=0)
    total = partial_sums(jnp.concatenate([total, jnp.concatenate([there, there], axis=1)], axis=0), "gz")
    basis = basis_half(behind(odd, total[0]), own, top, 0, None)
    total = total[-1]
    bottom = bottom_factor(total[:count], top, scale)
    here, cross = total[count : 2 * count, :count], total[count : 2 * count, count:]
    projected = project(jnp.concatenate([here, cross, total[2 * count :, :count]]), top, bottom, scale)
    basis = basis_half(odd, own + other, bottom, 1, basis)
    return basis[None], projected[None]


def solution(mesh):
    in_specs = (
        P("cuts", None, "gz", None, None),
        P("gz", None, None),
        P("cuts"),
        P("cuts"),
        P("cuts", None),
    )
    out_specs = (P("cuts", None, "gz", None, None), P("cuts", None, None))
    return jax.shard_map(body, mesh=mesh, in_specs=in_specs, out_specs=out_specs, check_vma=False)
```

```python
import functools

import jax
import jax.numpy as jnp
from jax import lax
from jax.experimental import pallas as pl
from jax.experimental.pallas import tpu as pltpu
from jax.sharding import PartitionSpec as P

F32 = jnp.float32
GROUP = 8
ROWS = 8
SPAN = 64
VMEM = pl.BlockSpec(memory_space=pltpu.VMEM)
SMEM = pl.BlockSpec(memory_space=pltpu.SMEM)
PARAMS = pltpu.CompilerParams(vmem_limit_bytes=24 * 1024 * 1024)

TERMS = ((2, 0), (1, 1), (0, 2), (1, 0), (0, 1), (0, 0))


def three_parts(value):
    parts = []
    for _ in range(3):
        parts.append(value.astype(jnp.bfloat16))
        value = value - parts[-1].astype(F32)
    return parts


def dot_wide(left, right):
    m, n = left.shape[0], right.shape[0]
    terms = lax.dot_general(
        jnp.concatenate(three_parts(left), axis=0),
        jnp.concatenate(three_parts(right), axis=0),
        (((1,), (1,)), ((), ())),
        preferred_element_type=F32,
    )
    return sum(terms[i * m : (i + 1) * m, j * n : (j + 1) * n] for i, j in TERMS)


def dot_tall(left, right):
    lefts, rights = three_parts(left), three_parts(right)
    return jnp.dot(
        jnp.concatenate([lefts[i] for i, _ in TERMS], axis=1),
        jnp.concatenate([rights[j] for _, j in TERMS], axis=0),
        preferred_element_type=F32,
    )


def dot_nt(left, right):
    return lax.dot_general(
        left, right, (((1,), (1,)), ((), ())), precision=lax.Precision.HIGHEST, preferred_element_type=F32
    )


def dot_nn(left, right):
    return jnp.dot(left, right, precision=lax.Precision.HIGHEST, preferred_element_type=F32)


def struct(*shape):
    return jax.ShapeDtypeStruct(shape, F32)


def cost(flops, nbytes):
    return pl.CostEstimate(flops=int(flops), bytes_accessed=int(nbytes), transcendentals=0)


SMALL = cost(1000, 1000)


def chunk_kernel(odd_ref, field0, field1, onsite_ref, out):
    size_x = field0.shape[2]
    for layer, source in enumerate((field0, field1)):
        flat = source.reshape(GROUP * size_x, source.shape[3])
        for j in range(size_x):
            out[layer * size_x + j] = flat[pl.ds(j, GROUP, stride=size_x), :]
    for j in range(out.shape[0] - 2 * size_x):
        out[2 * size_x + j] = onsite_ref[0, j * GROUP : (j + 1) * GROUP, :]


def to_chunk(field, onsite, odd, which):
    _, layers, size_x, size_y = field.shape
    rows = layers * size_x + (size_x // GROUP if which == 0 else 0)
    return pl.pallas_call(
        chunk_kernel,
        grid_spec=pltpu.PrefetchScalarGridSpec(
            num_scalar_prefetch=1,
            grid=(1,),
            in_specs=[
                pl.BlockSpec((GROUP, 1, size_x, size_y), lambda b, odd: (which, odd[0], 0, 0)),
                pl.BlockSpec((GROUP, 1, size_x, size_y), lambda b, odd: (which, 1 - odd[0], 0, 0)),
                pl.BlockSpec((1, size_x, size_y), lambda b, odd: (odd[0], 0, 0)),
            ],
            out_specs=pl.BlockSpec((rows, GROUP, size_y), lambda b, odd: (0, 0, 0)),
        ),
        out_shape=struct(rows, GROUP, size_y),
        compiler_params=PARAMS,
        cost_estimate=SMALL,
        name="to_chunk",
    )(odd, field, field, onsite)


def beside_in_y(value):
    lane = lax.broadcasted_iota(jnp.int32, value.shape, 1)
    size = value.shape[1]
    left = jnp.where(lane > 0, pltpu.roll(value, 1, 1), 0.0)
    right = jnp.where(lane < size - 1, pltpu.roll(value, size - 1, 1), 0.0)
    return left + right


def beside(ref, x, first, last):
    size_x = ref.shape[0]
    low = ref[x - 1] if first is None else jnp.where(first, ref[jnp.maximum(x - 1, 0)], 0.0)
    high = ref[x + 1] if last is None else jnp.where(last, ref[jnp.minimum(x + 1, size_x - 1)], 0.0)
    return (low + high) + beside_in_y(ref[x])


def over_rows(size_x, step):
    blocks = size_x // ROWS

    def wrapped(block, _):
        for i in range(ROWS):
            first = block > 0 if i == 0 else None
            last = block < blocks - 1 if i == ROWS - 1 else None
            step(block * ROWS + i, first, last)
        return 0

    lax.fori_loop(0, blocks, wrapped, 0)


def layers_of(ref, size_x):
    return ref.at[pl.ds(0, size_x)], ref.at[pl.ds(size_x, size_x)]


def row_of(site, x):
    return site[pl.ds(x, 1), :]


def factors(center, inv_half, cheb):
    h = inv_half[0]
    return center[0], cheb[0, 0] - cheb[0, 2], cheb[0, 1] * h, 2.0 * cheb[0, 2] * h * h


def local_kernel(token, center, inv_half, cheb, own, near, ons, ons_near, out, once, inner):
    size_x = once.shape[0]
    middle, a, b, g = factors(center, inv_half, cheb)
    own0, own1 = layers_of(own, size_x)
    near0, near1 = layers_of(near, size_x)
    out0, out1 = layers_of(out, size_x)

    def layer(here, sides, beyond, site, side_sites, result):
        def first(x, top, end):
            around = sum(side[x] for side in sides)
            t = (row_of(site, x) - middle) * here[x] - beside(here, x, top, end) - around
            once[x] = t
            inner[x] = t - around

        def second(x, top, end):
            t = once[x]
            twice = (row_of(site, x) - middle) * t - beside(inner, x, top, end)
            for side, energies in zip(sides, side_sites):
                twice = twice - (row_of(energies, x) - middle) * side[x]
            twice = twice + 2.0 * here[x] + beyond[x]
            result[x] = a * here[x] + b * t + g * twice

        over_rows(size_x, first)
        over_rows(size_x, second)

    layer(own1, (own0, near1), near0, ons.at[1], (ons.at[0], ons_near), out1)
    layer(own0, (own1,), near1, ons.at[0], (ons.at[1],), out0)


def filter_local(token, scalars, own, near, ons, ons_near):
    _, size_x, size_y = ons.shape
    layer = pltpu.VMEM((size_x, GROUP, size_y), F32)
    return pl.pallas_call(
        local_kernel,
        in_specs=[SMEM] * 4 + [VMEM] * 4,
        out_specs=VMEM,
        out_shape=struct(2 * size_x, GROUP, size_y),
        scratch_shapes=[layer, layer],
        compiler_params=PARAMS,
        cost_estimate=SMALL,
        name="filter_local",
    )(token, *scalars, own, near, ons, ons_near)


def far_kernel(odd_ref, center, inv_half, cheb, base, far, ons, ons_far, out, pay):
    _, size_x, size_y = ons.shape
    middle, a, b, g = factors(center, inv_half, cheb)
    base0, base1 = layers_of(base, size_x)
    far0, far1 = layers_of(far, size_x)
    out0, out1 = layers_of(out, size_x)
    shift = b - 2.0 * g * middle

    def step(x, top, end):
        value = far0[x]
        site = g * (row_of(ons.at[0], x) + row_of(ons_far, x)) + shift
        out0[x] = base0[x] + ((2.0 * g) * beside(far0, x, top, end) - site * value + g * far1[x])
        out1[x] = base1[x] + g * value

    over_rows(size_x, step)
    half = size_x // 2
    start = (1 - odd_ref[0]) * half

    def copy(block, _):
        pay[pl.ds(block * ROWS, ROWS)] = out[pl.ds(start + block * ROWS, ROWS)]
        return 0

    lax.fori_loop(0, half // ROWS, copy, 0)


def filter_far(odd, scalars, base, far, ons, ons_far):
    _, size_x, size_y = ons.shape
    return pl.pallas_call(
        far_kernel,
        in_specs=[SMEM] * 4 + [VMEM] * 4,
        out_specs=[VMEM] * 2,
        out_shape=[struct(2 * size_x, GROUP, size_y), struct(size_x // 2, GROUP, size_y)],
        compiler_params=PARAMS,
        cost_estimate=SMALL,
        name="filter_far",
    )(odd, *scalars, base, far, ons, ons_far)


def image_kernel(token, own, beyond, ons, out):
    size_x = ons.shape[1]
    own0, own1 = layers_of(own, size_x)
    out0, out1 = layers_of(out, size_x)

    def step(x, top, end):
        value0, value1 = own0[x], own1[x]
        out0[x] = row_of(ons.at[0], x) * value0 - beside(own0, x, top, end) - value1
        out1[x] = row_of(ons.at[1], x) * value1 - beside(own1, x, top, end) - (value0 + beyond[size_x + x])

    over_rows(size_x, step)


def stage_kernel(token, center, inv_half, cheb, own, beyond, mine, near, ons, ons_near, image, base, once, inner):
    image_kernel(token, own, beyond, ons, image)
    local_kernel(token, center, inv_half, cheb, mine, near, ons, ons_near, base, once, inner)


def stage(token, scalars, own, beyond, mine, near, ons, ons_near):
    _, size_x, size_y = ons.shape
    layer = pltpu.VMEM((size_x, GROUP, size_y), F32)
    chunk = struct(2 * size_x, GROUP, size_y)
    return pl.pallas_call(
        stage_kernel,
        in_specs=[SMEM] * 4 + [VMEM] * 6,
        out_specs=[VMEM] * 2,
        out_shape=[chunk, chunk],
        scratch_shapes=[layer, layer],
        compiler_params=PARAMS,
        cost_estimate=SMALL,
        name="stage",
    )(token, *scalars, own, beyond, mine, near, ons, ons_near)


def image_chunk(token, own, beyond, ons):
    return pl.pallas_call(
        image_kernel,
        in_specs=[SMEM] + [VMEM] * 3,
        out_specs=VMEM,
        out_shape=struct(*own.shape),
        compiler_params=PARAMS,
        cost_estimate=SMALL,
        name="image_chunk",
    )(token, own, beyond, ons)


def wide(refs, x, rows):
    return jnp.concatenate([jnp.concatenate([ref[x + i] for i in range(rows)], axis=1) for ref in refs], axis=0)


def products_kernel(lefts, itself, token, *refs):
    left, right, out = refs[:lefts], refs[lefts:-1], refs[-1]
    rows = left[0].shape[0]

    @pl.when(pl.program_id(0) == 0)
    def _():
        out[...] = jnp.zeros_like(out)

    here, there = wide(left, 0, rows), wide(right, 0, rows)
    if itself:
        there = jnp.concatenate([here, there], axis=0)
    out[...] += dot_wide(here, there)


def products(token, left, right, itself=False):
    rows_all, _, size_y = left[0].shape
    part = pl.BlockSpec((SPAN, GROUP, size_y), lambda b, token: (b, 0, 0))
    columns = len(right) + (len(left) if itself else 0)
    shape = (len(left) * GROUP, columns * GROUP)
    return pl.pallas_call(
        functools.partial(products_kernel, len(left), itself),
        grid_spec=pltpu.PrefetchScalarGridSpec(
            num_scalar_prefetch=1,
            grid=(rows_all // SPAN,),
            in_specs=[part] * (len(left) + len(right)),
            out_specs=pl.BlockSpec(shape, lambda b, token: (0, 0)),
        ),
        out_shape=struct(*shape),
        compiler_params=PARAMS,
        cost_estimate=SMALL,
        name="products",
    )(token, *left, *right)


def border_kernel(count, odd_ref, *refs):
    own, other, halos, next_halos, out = refs[:count], refs[count : 2 * count], refs[-5:-3], refs[-3:-1], refs[-1]
    half = own[0].shape[0]

    def step(block, total):
        x = block * SPAN

        def beyond(stacks):
            return wide([stack.at[i] for stack in stacks for i in range(stack.shape[0])], x, SPAN)

        left = jnp.concatenate([wide(other, x, SPAN), beyond(next_halos)], axis=1)
        return total + dot_wide(left, jnp.concatenate([beyond(halos), wide(own, x, SPAN)], axis=1))

    out[...] = lax.fori_loop(0, half // SPAN, step, jnp.zeros(out.shape, F32))


def own_border_kernel(count, odd_ref, *refs):
    own, halos, out = refs[:count], refs[count:-1], refs[-1]
    half = own[0].shape[0]

    def step(block, total):
        x = block * SPAN
        there = wide([stack.at[i] for stack in halos for i in range(stack.shape[0])], x, SPAN)
        return total + dot_wide(wide(own, x, SPAN), there)

    out[...] = lax.fori_loop(0, half // SPAN, step, jnp.zeros(out.shape, F32))


def border_products(odd, kernel, layers, halos):
    _, half, _, size_y = halos[0].shape
    size = sum(stack.shape[0] for stack in halos[:2]) * GROUP
    mine = pl.BlockSpec((half, GROUP, size_y), lambda b, odd: (odd[0], 0, 0))
    theirs = [pl.BlockSpec(stack.shape, lambda b, odd: (0, 0, 0, 0)) for stack in halos]
    return pl.pallas_call(
        functools.partial(kernel, size // GROUP),
        grid_spec=pltpu.PrefetchScalarGridSpec(
            num_scalar_prefetch=1,
            grid=(1,),
            in_specs=[mine] * len(layers) + theirs,
            out_specs=pl.BlockSpec((size, size), lambda b, odd: (0, 0)),
        ),
        out_shape=struct(size, size),
        compiler_params=PARAMS,
        cost_estimate=SMALL,
        name="border_products",
    )(odd, *layers, *halos)


def inverse_factor(matrix):
    size = matrix.shape[0]
    row = lax.broadcasted_iota(jnp.int32, (size, size), 0)
    col = lax.broadcasted_iota(jnp.int32, (size, size), 1)
    identity = jnp.where(row == col, 1.0, 0.0)
    work = jnp.concatenate([matrix, identity], axis=1)
    below = lax.broadcasted_iota(jnp.int32, work.shape, 0)
    for j in range(size):
        pivot = work[j : j + 1, :]
        ratio = work[:, j : j + 1] / pivot[:, j : j + 1]
        work = work - jnp.where(below > j, ratio, 0.0) * pivot
    pivots = jnp.sum(work[:, :size] * identity, axis=1, keepdims=True)
    return work[:, size:] / jnp.sqrt(pivots)


def with_shift(gram, scale):
    row = lax.broadcasted_iota(jnp.int32, gram.shape, 0)
    col = lax.broadcasted_iota(jnp.int32, gram.shape, 1)
    return gram * scale + jnp.where(row == col, 0.25, 0.0)


def factor_kernel(scale, sums, inverse_out, projected):
    size = sums.shape[0] // 3
    own, cross, other = (sums[i * size : (i + 1) * size, :] for i in range(3))
    top = inverse_factor(with_shift(own[:, :size], scale))
    low = dot_nt(cross[:, :size] * scale, top)
    inverse = inverse_factor(with_shift(other[:, :size], scale) - dot_nt(low, low))
    side = -dot_nn(inverse, dot_nn(low, top))
    whole = jnp.concatenate(
        [jnp.concatenate([top, jnp.zeros_like(top)], axis=1), jnp.concatenate([side, inverse], axis=1)], axis=0
    )
    inverse_out[...] = whole
    here, mixed, there = own[:, size:], cross[:, size:], other[:, size:]
    upper = jnp.concatenate([here + here.T, mixed.T], axis=1)
    lower = jnp.concatenate([mixed, there + there.T], axis=1)
    matrix = jnp.concatenate([upper, lower], axis=0) * (0.5 * scale)
    projected[...] = dot_nt(dot_nn(whole, matrix), whole)


def factor(sums, scale):
    size = sums.shape[0] // 3
    return pl.pallas_call(
        functools.partial(factor_kernel, scale),
        in_specs=[VMEM],
        out_specs=[VMEM] * 2,
        out_shape=[struct(2 * size, 2 * size)] * 2,
        compiler_params=PARAMS,
        cost_estimate=SMALL,
        name="factor",
    )(sums)


def basis_kernel(count, odd_ref, *refs):
    parts, coef, out = refs[:count], refs[count], refs[-1]
    rows, _, size_y = parts[0].shape
    result = dot_tall(coef[...], wide(parts, 0, rows))
    for v in range(0, out.shape[0], GROUP):
        for j in range(0, rows, GROUP):
            pieces = [result[v : v + GROUP, (j + i) * size_y : (j + i + 1) * size_y] for i in range(GROUP)]
            out[v : v + GROUP, 0, j : j + GROUP, :] = jnp.swapaxes(jnp.stack(pieces, axis=0), 0, 1)


def basis_of(odd, parts, coef):
    rows_all, _, size_y = parts[0].shape
    layers, rows = 2, SPAN
    size_x = rows_all // layers
    blocks = size_x // rows
    size = coef.shape[0]
    part = pl.BlockSpec((rows, GROUP, size_y), lambda s, b, odd: (s * blocks + b, 0, 0))
    return pl.pallas_call(
        functools.partial(basis_kernel, len(parts)),
        grid_spec=pltpu.PrefetchScalarGridSpec(
            num_scalar_prefetch=1,
            grid=(layers, blocks),
            in_specs=[part] * len(parts) + [pl.BlockSpec(coef.shape, lambda s, b, odd: (0, 0))],
            out_specs=pl.BlockSpec((size, 1, rows, size_y), lambda s, b, odd: (0, (s + odd[0]) % 2, b, 0)),
        ),
        out_shape=struct(size, layers, size_x, size_y),
        compiler_params=PARAMS,
        cost_estimate=SMALL,
        name="basis_of",
    )(odd, *parts, coef)


def behind(value, *others):
    return lax.optimization_barrier((value, *others))[0]


def partial_sums(value, axis, *others):
    size = lax.axis_size(axis)
    if size & (size - 1):
        return [lax.psum(value, axis)]
    sums = []
    step = 1
    while step < size:
        value = value + lax.ppermute(value, axis, [(i, i ^ step) for i in range(size)])
        if step == 1:
            value = behind(value, *others)
        sums.append(value)
        step *= 2
    return sums


def body(vectors, onsite, center, inv_half, cheb_coef):
    field = vectors[0]
    count, layers, size_x, size_y = field.shape
    ring = lax.axis_size("gz")
    cuts = lax.axis_size("cuts")
    scale = 1.0 / (layers * ring * size_x * size_y)
    odd = (lax.axis_index("gz") % 2).astype(jnp.int32)[None]
    across = [(i, (i + 1) % ring if i % 2 else (i - 1) % ring) for i in range(ring)]
    pair = [(i, i ^ 1) for i in range(ring)]
    left = [(i, i - 1) for i in range(1, cuts)]

    def inter_swap(value):
        return lax.ppermute(value, "gz", across)

    def intra_swap(value):
        return lax.ppermute(value, "gz", pair)

    def from_next(value):
        return lax.ppermute(value, "cuts", left)

    scalars = (center, inv_half, cheb_coef)
    ons = jnp.where(odd[0] == 0, onsite, onsite[::-1])
    groups = range(count // GROUP)

    mine, near, far = [], [], []
    token = odd
    for i in groups:
        mine.append(to_chunk(field, onsite, behind(odd, token), i))
        token = mine[-1]
    rows = layers * size_x
    near = [intra_swap(mine[0])]
    ons_near = intra_swap(ons[1])
    for i in groups[1:]:
        near.append(intra_swap(behind(mine[i], near[-1])))
    far = [inter_swap(mine[0]), inter_swap(behind(mine[1], near[0]))]

    def local(i, *tokens):
        return filter_local(behind(odd, *tokens), scalars, mine[i], near[i], ons, ons_near)

    base = local(0, mine[-1])
    far[0] = behind(far[0], base)
    ons_far = far[0][rows:].reshape(size_x, size_y)
    own, other, image, pay, beyond = [], [], [], [], []
    last = len(groups) - 1
    for i in groups:
        out, half = filter_far(behind(odd, base), scalars, base, far[i], ons, ons_far)
        own.append(out)
        pay.append(half)
        other.append(from_next(out))
        beyond.append(intra_swap(out))
        if i + 2 <= last:
            far.append(inter_swap(behind(mine[i + 2], far[i])))
        token = behind(odd, out, *other[i - 1 : i]) if i else behind(odd, out)
        if i == 0:
            base = local(1, token)
        elif i < last:
            done, base = stage(token, scalars, own[i - 1], beyond[i - 1], mine[i + 1], near[i + 1], ons, ons_near)
            image.append(done)
        else:
            image.append(image_chunk(token, own[i - 1], beyond[i - 1], ons))
            image.append(image_chunk(behind(odd, image[-1]), own[i], beyond[i], ons))

    middle = (last + 1) // 2
    halo0 = [inter_swap(behind(jnp.stack(pay[:middle]), own[-1])), inter_swap(jnp.stack(pay[middle:]))]
    both = products(odd, own, image, True)
    start = (1 - odd[0]) * (size_x // 2)
    next_pay = [lax.dynamic_slice_in_dim(behind(value, both), start, size_x // 2, 0) for value in other[:middle]]
    next_pay = inter_swap(jnp.stack(next_pay))
    border = border_products(behind(odd, both), own_border_kernel, own, halo0)
    here = jnp.concatenate([both[:, :count], both[:, count:] - 2.0 * border], axis=1)
    next_halo0 = [next_pay, from_next(behind(halo0[1], both))]
    there = from_next(here)
    cross = products(behind(odd, border), other, own + image)
    border = border_products(behind(odd, cross, there), border_kernel, own + other, halo0 + next_halo0)
    cross = jnp.concatenate([cross[:, :count], 2.0 * (cross[:, count:] - border)], axis=1)
    sums = partial_sums(jnp.concatenate([here, cross, there], axis=0), "gz")[-1]
    inverse, projected = factor(sums, scale)
    basis = basis_of(odd, own + other, inverse)
    return basis[None], projected[None]


def solution(mesh):
    in_specs = (
        P("cuts", None, "gz", None, None),
        P("gz", None, None),
        P("cuts"),
        P("cuts"),
        P("cuts", None),
    )
    out_specs = (P("cuts", None, "gz", None, None), P("cuts", None, None))
    return jax.shard_map(body, mesh=mesh, in_specs=in_specs, out_specs=out_specs, check_vma=False)
```

```python
import functools

import jax
import jax.numpy as jnp
from jax import lax
from jax.experimental import pallas as pl
from jax.experimental.pallas import tpu as pltpu
from jax.sharding import PartitionSpec as P

F32 = jnp.float32
GROUP = 8
ROWS = 8
SPAN = 64
VMEM = pl.BlockSpec(memory_space=pltpu.VMEM)
SMEM = pl.BlockSpec(memory_space=pltpu.SMEM)
PARAMS = pltpu.CompilerParams(vmem_limit_bytes=24 * 1024 * 1024)

TERMS = ((2, 0), (1, 1), (0, 2), (1, 0), (0, 1), (0, 0))


def three_parts(value):
    parts = []
    for _ in range(3):
        parts.append(value.astype(jnp.bfloat16))
        value = value - parts[-1].astype(F32)
    return parts


def dot_wide(left, right):
    m, n = left.shape[0], right.shape[0]
    terms = lax.dot_general(
        jnp.concatenate(three_parts(left), axis=0),
        jnp.concatenate(three_parts(right), axis=0),
        (((1,), (1,)), ((), ())),
        preferred_element_type=F32,
    )
    return sum(terms[i * m : (i + 1) * m, j * n : (j + 1) * n] for i, j in TERMS)


def dot_tall(left, right):
    lefts, rights = three_parts(left), three_parts(right)
    return jnp.dot(
        jnp.concatenate([lefts[i] for i, _ in TERMS], axis=1),
        jnp.concatenate([rights[j] for _, j in TERMS], axis=0),
        preferred_element_type=F32,
    )


def dot_nt(left, right):
    return lax.dot_general(
        left, right, (((1,), (1,)), ((), ())), precision=lax.Precision.HIGHEST, preferred_element_type=F32
    )


def dot_nn(left, right):
    return jnp.dot(left, right, precision=lax.Precision.HIGHEST, preferred_element_type=F32)


def struct(*shape):
    return jax.ShapeDtypeStruct(shape, F32)


def cost(flops, nbytes):
    return pl.CostEstimate(flops=int(flops), bytes_accessed=int(nbytes), transcendentals=0)


SMALL = cost(1000, 1000)


def chunk_kernel(odd_ref, field0, field1, onsite_ref, out):
    size_x = field0.shape[2]
    for layer, source in enumerate((field0, field1)):
        flat = source.reshape(GROUP * size_x, source.shape[3])
        for j in range(size_x):
            out[layer * size_x + j] = flat[pl.ds(j, GROUP, stride=size_x), :]
    for j in range(out.shape[0] - 2 * size_x):
        out[2 * size_x + j] = onsite_ref[0, j * GROUP : (j + 1) * GROUP, :]


def to_chunk(field, onsite, odd, which):
    _, layers, size_x, size_y = field.shape
    rows = layers * size_x + (size_x // GROUP if which == 0 else 0)
    return pl.pallas_call(
        chunk_kernel,
        grid_spec=pltpu.PrefetchScalarGridSpec(
            num_scalar_prefetch=1,
            grid=(1,),
            in_specs=[
                pl.BlockSpec((GROUP, 1, size_x, size_y), lambda b, odd: (which, odd[0], 0, 0)),
                pl.BlockSpec((GROUP, 1, size_x, size_y), lambda b, odd: (which, 1 - odd[0], 0, 0)),
                pl.BlockSpec((1, size_x, size_y), lambda b, odd: (odd[0], 0, 0)),
            ],
            out_specs=pl.BlockSpec((rows, GROUP, size_y), lambda b, odd: (0, 0, 0)),
        ),
        out_shape=struct(rows, GROUP, size_y),
        compiler_params=PARAMS,
        cost_estimate=SMALL,
        name="to_chunk",
    )(odd, field, field, onsite)


def beside_in_y(value):
    lane = lax.broadcasted_iota(jnp.int32, value.shape, 1)
    size = value.shape[1]
    left = jnp.where(lane > 0, pltpu.roll(value, 1, 1), 0.0)
    right = jnp.where(lane < size - 1, pltpu.roll(value, size - 1, 1), 0.0)
    return left + right


def beside(ref, x, first, last):
    size_x = ref.shape[0]
    low = ref[x - 1] if first is None else jnp.where(first, ref[jnp.maximum(x - 1, 0)], 0.0)
    high = ref[x + 1] if last is None else jnp.where(last, ref[jnp.minimum(x + 1, size_x - 1)], 0.0)
    return (low + high) + beside_in_y(ref[x])


def over_rows(size_x, step):
    blocks = size_x // ROWS

    def wrapped(block, _):
        for i in range(ROWS):
            first = block > 0 if i == 0 else None
            last = block < blocks - 1 if i == ROWS - 1 else None
            step(block * ROWS + i, first, last)
        return 0

    lax.fori_loop(0, blocks, wrapped, 0)


def layers_of(ref, size_x):
    return ref.at[pl.ds(0, size_x)], ref.at[pl.ds(size_x, size_x)]


def row_of(site, x):
    return site[pl.ds(x, 1), :]


def factors(center, inv_half, cheb):
    h = inv_half[0]
    return center[0], cheb[0, 0] - cheb[0, 2], cheb[0, 1] * h, 2.0 * cheb[0, 2] * h * h


def local_kernel(token, center, inv_half, cheb, own, near, ons, ons_near, out, once, inner):
    size_x = once.shape[0]
    middle, a, b, g = factors(center, inv_half, cheb)
    own0, own1 = layers_of(own, size_x)
    near0, near1 = layers_of(near, size_x)
    out0, out1 = layers_of(out, size_x)

    def layer(here, sides, beyond, site, side_sites, result):
        def first(x, top, end):
            around = sum(side[x] for side in sides)
            t = (row_of(site, x) - middle) * here[x] - beside(here, x, top, end) - around
            once[x] = t
            inner[x] = t - around

        def second(x, top, end):
            t = once[x]
            twice = (row_of(site, x) - middle) * t - beside(inner, x, top, end)
            for side, energies in zip(sides, side_sites):
                twice = twice - (row_of(energies, x) - middle) * side[x]
            twice = twice + 2.0 * here[x] + beyond[x]
            result[x] = a * here[x] + b * t + g * twice

        over_rows(size_x, first)
        over_rows(size_x, second)

    layer(own1, (own0, near1), near0, ons.at[1], (ons.at[0], ons_near), out1)
    layer(own0, (own1,), near1, ons.at[0], (ons.at[1],), out0)


def filter_local(token, scalars, own, near, ons, ons_near):
    _, size_x, size_y = ons.shape
    layer = pltpu.VMEM((size_x, GROUP, size_y), F32)
    return pl.pallas_call(
        local_kernel,
        in_specs=[SMEM] * 4 + [VMEM] * 4,
        out_specs=VMEM,
        out_shape=struct(2 * size_x, GROUP, size_y),
        scratch_shapes=[layer, layer],
        compiler_params=PARAMS,
        cost_estimate=SMALL,
        name="filter_local",
    )(token, *scalars, own, near, ons, ons_near)


def far_kernel(odd_ref, center, inv_half, cheb, base, far, ons, ons_far, out, pay):
    _, size_x, size_y = ons.shape
    middle, a, b, g = factors(center, inv_half, cheb)
    base0, base1 = layers_of(base, size_x)
    far0, far1 = layers_of(far, size_x)
    out0, out1 = layers_of(out, size_x)
    shift = b - 2.0 * g * middle

    def step(x, top, end):
        value = far0[x]
        site = g * (row_of(ons.at[0], x) + row_of(ons_far, x)) + shift
        out0[x] = base0[x] + ((2.0 * g) * beside(far0, x, top, end) - site * value + g * far1[x])
        out1[x] = base1[x] + g * value

    over_rows(size_x, step)
    half = size_x // 2
    start = (1 - odd_ref[0]) * half

    def copy(block, _):
        pay[pl.ds(block * ROWS, ROWS)] = out[pl.ds(start + block * ROWS, ROWS)]
        return 0

    lax.fori_loop(0, half // ROWS, copy, 0)


def filter_far(odd, scalars, base, far, ons, ons_far):
    _, size_x, size_y = ons.shape
    return pl.pallas_call(
        far_kernel,
        in_specs=[SMEM] * 4 + [VMEM] * 4,
        out_specs=[VMEM] * 2,
        out_shape=[struct(2 * size_x, GROUP, size_y), struct(size_x // 2, GROUP, size_y)],
        compiler_params=PARAMS,
        cost_estimate=SMALL,
        name="filter_far",
    )(odd, *scalars, base, far, ons, ons_far)


def image_kernel(token, own, beyond, ons, out):
    size_x = ons.shape[1]
    own0, own1 = layers_of(own, size_x)
    out0, out1 = layers_of(out, size_x)

    def step(x, top, end):
        value0, value1 = own0[x], own1[x]
        out0[x] = row_of(ons.at[0], x) * value0 - beside(own0, x, top, end) - value1
        out1[x] = row_of(ons.at[1], x) * value1 - beside(own1, x, top, end) - (value0 + beyond[size_x + x])

    over_rows(size_x, step)


def stage_kernel(token, center, inv_half, cheb, own, beyond, mine, near, ons, ons_near, image, base, once, inner):
    image_kernel(token, own, beyond, ons, image)
    local_kernel(token, center, inv_half, cheb, mine, near, ons, ons_near, base, once, inner)


def stage(token, scalars, own, beyond, mine, near, ons, ons_near):
    _, size_x, size_y = ons.shape
    layer = pltpu.VMEM((size_x, GROUP, size_y), F32)
    chunk = struct(2 * size_x, GROUP, size_y)
    return pl.pallas_call(
        stage_kernel,
        in_specs=[SMEM] * 4 + [VMEM] * 6,
        out_specs=[VMEM] * 2,
        out_shape=[chunk, chunk],
        scratch_shapes=[layer, layer],
        compiler_params=PARAMS,
        cost_estimate=SMALL,
        name="stage",
    )(token, *scalars, own, beyond, mine, near, ons, ons_near)


def image_chunk(token, own, beyond, ons):
    return pl.pallas_call(
        image_kernel,
        in_specs=[SMEM] + [VMEM] * 3,
        out_specs=VMEM,
        out_shape=struct(*own.shape),
        compiler_params=PARAMS,
        cost_estimate=SMALL,
        name="image_chunk",
    )(token, own, beyond, ons)


def wide(refs, x, rows):
    return jnp.concatenate([jnp.concatenate([ref[x + i] for i in range(rows)], axis=1) for ref in refs], axis=0)


def products_kernel(lefts, itself, token, *refs):
    left, right, out = refs[:lefts], refs[lefts:-1], refs[-1]
    rows = left[0].shape[0]

    @pl.when(pl.program_id(0) == 0)
    def _():
        out[...] = jnp.zeros_like(out)

    here, there = wide(left, 0, rows), wide(right, 0, rows)
    if itself:
        there = jnp.concatenate([here, there], axis=0)
    out[...] += dot_wide(here, there)


def products(token, left, right, itself=False):
    rows_all, _, size_y = left[0].shape
    part = pl.BlockSpec((SPAN, GROUP, size_y), lambda b, token: (b, 0, 0))
    columns = len(right) + (len(left) if itself else 0)
    shape = (len(left) * GROUP, columns * GROUP)
    return pl.pallas_call(
        functools.partial(products_kernel, len(left), itself),
        grid_spec=pltpu.PrefetchScalarGridSpec(
            num_scalar_prefetch=1,
            grid=(rows_all // SPAN,),
            in_specs=[part] * (len(left) + len(right)),
            out_specs=pl.BlockSpec(shape, lambda b, token: (0, 0)),
        ),
        out_shape=struct(*shape),
        compiler_params=PARAMS,
        cost_estimate=SMALL,
        name="products",
    )(token, *left, *right)


def border_kernel(count, odd_ref, *refs):
    own, other, halos, next_halos, out = refs[:count], refs[count : 2 * count], refs[-5:-3], refs[-3:-1], refs[-1]
    half = own[0].shape[0]

    def step(block, total):
        x = block * SPAN

        def beyond(stacks):
            return wide([stack.at[i] for stack in stacks for i in range(stack.shape[0])], x, SPAN)

        left = jnp.concatenate([wide(other, x, SPAN), beyond(next_halos)], axis=1)
        return total + dot_wide(left, jnp.concatenate([beyond(halos), wide(own, x, SPAN)], axis=1))

    out[...] = lax.fori_loop(0, half // SPAN, step, jnp.zeros(out.shape, F32))


def own_border_kernel(count, odd_ref, *refs):
    own, halos, out = refs[:count], refs[count:-1], refs[-1]
    half = own[0].shape[0]

    def step(block, total):
        x = block * SPAN
        there = wide([stack.at[i] for stack in halos for i in range(stack.shape[0])], x, SPAN)
        return total + dot_wide(wide(own, x, SPAN), there)

    out[...] = lax.fori_loop(0, half // SPAN, step, jnp.zeros(out.shape, F32))


def border_products(odd, kernel, layers, halos):
    _, half, _, size_y = halos[0].shape
    size = sum(stack.shape[0] for stack in halos[:2]) * GROUP
    mine = pl.BlockSpec((half, GROUP, size_y), lambda b, odd: (odd[0], 0, 0))
    theirs = [pl.BlockSpec(stack.shape, lambda b, odd: (0, 0, 0, 0)) for stack in halos]
    return pl.pallas_call(
        functools.partial(kernel, size // GROUP),
        grid_spec=pltpu.PrefetchScalarGridSpec(
            num_scalar_prefetch=1,
            grid=(1,),
            in_specs=[mine] * len(layers) + theirs,
            out_specs=pl.BlockSpec((size, size), lambda b, odd: (0, 0)),
        ),
        out_shape=struct(size, size),
        compiler_params=PARAMS,
        cost_estimate=SMALL,
        name="border_products",
    )(odd, *layers, *halos)


def inverse_factor(matrix):
    size = matrix.shape[0]
    row = lax.broadcasted_iota(jnp.int32, (size, size), 0)
    col = lax.broadcasted_iota(jnp.int32, (size, size), 1)
    identity = jnp.where(row == col, 1.0, 0.0)
    work = jnp.concatenate([matrix, identity], axis=1)
    below = lax.broadcasted_iota(jnp.int32, work.shape, 0)
    for j in range(0, size, GROUP):
        columns = [jnp.broadcast_to(work[:, j + k : j + k + 1], work.shape) for k in range(GROUP)]
        rows = [work[j + k : j + k + 1, :] for k in range(GROUP)]
        steps = []
        for k in range(GROUP):
            steps.append(rows[k] / columns[k][j + k : j + k + 1, :])
            for m in range(k + 1, GROUP):
                share = columns[k][j + m : j + m + 1, :]
                rows[m] = rows[m] - share * steps[k]
                columns[m] = columns[m] - columns[k] * (share / columns[k][j + k : j + k + 1, :])
        rest = work
        for k in range(GROUP):
            rest = rest - columns[k] * steps[k]
        for k in range(GROUP):
            rest = jnp.where(below == j + k, rows[k], rest)
        work = jnp.where(below < j, work, rest)
    pivots = jnp.sum(work[:, :size] * identity, axis=1, keepdims=True)
    return work[:, size:] / jnp.sqrt(pivots)


def with_shift(gram, scale):
    row = lax.broadcasted_iota(jnp.int32, gram.shape, 0)
    col = lax.broadcasted_iota(jnp.int32, gram.shape, 1)
    return gram * scale + jnp.where(row == col, 0.25, 0.0)


def factor_kernel(scale, sums, inverse_out, projected):
    size = sums.shape[0] // 3
    own, cross, other = (sums[i * size : (i + 1) * size, :] for i in range(3))
    top = inverse_factor(with_shift(own[:, :size], scale))
    low = dot_nt(cross[:, :size] * scale, top)
    inverse = inverse_factor(with_shift(other[:, :size], scale) - dot_nt(low, low))
    side = -dot_nn(inverse, dot_nn(low, top))
    whole = jnp.concatenate(
        [jnp.concatenate([top, jnp.zeros_like(top)], axis=1), jnp.concatenate([side, inverse], axis=1)], axis=0
    )
    inverse_out[...] = whole
    here, mixed, there = own[:, size:], cross[:, size:], other[:, size:]
    upper = jnp.concatenate([here + here.T, mixed.T], axis=1)
    lower = jnp.concatenate([mixed, there + there.T], axis=1)
    matrix = jnp.concatenate([upper, lower], axis=0) * (0.5 * scale)
    projected[...] = dot_nt(dot_nn(whole, matrix), whole)


def factor(sums, scale):
    size = sums.shape[0] // 3
    return pl.pallas_call(
        functools.partial(factor_kernel, scale),
        in_specs=[VMEM],
        out_specs=[VMEM] * 2,
        out_shape=[struct(2 * size, 2 * size)] * 2,
        compiler_params=PARAMS,
        cost_estimate=SMALL,
        name="factor",
    )(sums)


def basis_kernel(count, odd_ref, *refs):
    parts, coef, out = refs[:count], refs[count], refs[-1]
    rows, _, size_y = parts[0].shape
    result = dot_tall(coef[...], wide(parts, 0, rows))
    for v in range(0, out.shape[0], GROUP):
        for j in range(0, rows, GROUP):
            pieces = [result[v : v + GROUP, (j + i) * size_y : (j + i + 1) * size_y] for i in range(GROUP)]
            out[v : v + GROUP, 0, j : j + GROUP, :] = jnp.swapaxes(jnp.stack(pieces, axis=0), 0, 1)


def basis_of(odd, parts, coef):
    rows_all, _, size_y = parts[0].shape
    layers, rows = 2, SPAN
    size_x = rows_all // layers
    blocks = size_x // rows
    size = coef.shape[0]
    part = pl.BlockSpec((rows, GROUP, size_y), lambda s, b, odd: (s * blocks + b, 0, 0))
    return pl.pallas_call(
        functools.partial(basis_kernel, len(parts)),
        grid_spec=pltpu.PrefetchScalarGridSpec(
            num_scalar_prefetch=1,
            grid=(layers, blocks),
            in_specs=[part] * len(parts) + [pl.BlockSpec(coef.shape, lambda s, b, odd: (0, 0))],
            out_specs=pl.BlockSpec((size, 1, rows, size_y), lambda s, b, odd: (0, (s + odd[0]) % 2, b, 0)),
        ),
        out_shape=struct(size, layers, size_x, size_y),
        compiler_params=PARAMS,
        cost_estimate=SMALL,
        name="basis_of",
    )(odd, *parts, coef)


def behind(value, *others):
    return lax.optimization_barrier((value, *others))[0]


def partial_sums(value, axis, *others):
    size = lax.axis_size(axis)
    if size & (size - 1):
        return [lax.psum(value, axis)]
    sums = []
    step = 1
    while step < size:
        value = value + lax.ppermute(value, axis, [(i, i ^ step) for i in range(size)])
        if step == 1:
            value = behind(value, *others)
        sums.append(value)
        step *= 2
    return sums


def body(vectors, onsite, center, inv_half, cheb_coef):
    field = vectors[0]
    count, layers, size_x, size_y = field.shape
    ring = lax.axis_size("gz")
    cuts = lax.axis_size("cuts")
    scale = 1.0 / (layers * ring * size_x * size_y)
    odd = (lax.axis_index("gz") % 2).astype(jnp.int32)[None]
    across = [(i, (i + 1) % ring if i % 2 else (i - 1) % ring) for i in range(ring)]
    pair = [(i, i ^ 1) for i in range(ring)]
    left = [(i, i - 1) for i in range(1, cuts)]

    def inter_swap(value):
        return lax.ppermute(value, "gz", across)

    def intra_swap(value):
        return lax.ppermute(value, "gz", pair)

    def from_next(value):
        return lax.ppermute(value, "cuts", left)

    scalars = (center, inv_half, cheb_coef)
    ons = jnp.where(odd[0] == 0, onsite, onsite[::-1])
    groups = range(count // GROUP)

    mine, near, far = [], [], []
    token = odd
    for i in groups:
        mine.append(to_chunk(field, onsite, behind(odd, token), i))
        token = mine[-1]
    rows = layers * size_x
    near = [intra_swap(mine[0])]
    ons_near = intra_swap(ons[1])
    for i in groups[1:]:
        near.append(intra_swap(behind(mine[i], near[-1])))
    far = [inter_swap(mine[0]), inter_swap(behind(mine[1], near[0]))]

    def local(i, *tokens):
        return filter_local(behind(odd, *tokens), scalars, mine[i], near[i], ons, ons_near)

    base = local(0, mine[-1])
    far[0] = behind(far[0], base)
    ons_far = far[0][rows:].reshape(size_x, size_y)
    own, other, image, pay, beyond = [], [], [], [], []
    last = len(groups) - 1
    for i in groups:
        out, half = filter_far(behind(odd, base), scalars, base, far[i], ons, ons_far)
        own.append(out)
        pay.append(half)
        other.append(from_next(out))
        beyond.append(intra_swap(out))
        if i + 2 <= last:
            far.append(inter_swap(behind(mine[i + 2], far[i])))
        token = behind(odd, out, *other[i - 1 : i]) if i else behind(odd, out)
        if i == 0:
            base = local(1, token)
        elif i < last:
            done, base = stage(token, scalars, own[i - 1], beyond[i - 1], mine[i + 1], near[i + 1], ons, ons_near)
            image.append(done)
        else:
            image.append(image_chunk(token, own[i - 1], beyond[i - 1], ons))
            image.append(image_chunk(behind(odd, image[-1]), own[i], beyond[i], ons))

    middle = (last + 1) // 2
    halo0 = [inter_swap(behind(jnp.stack(pay[:middle]), own[-1])), inter_swap(jnp.stack(pay[middle:]))]
    both = products(odd, own, image, True)
    start = (1 - odd[0]) * (size_x // 2)
    next_pay = [lax.dynamic_slice_in_dim(behind(value, both), start, size_x // 2, 0) for value in other[:middle]]
    next_pay = inter_swap(jnp.stack(next_pay))
    border = border_products(behind(odd, both), own_border_kernel, own, halo0)
    here = jnp.concatenate([both[:, :count], both[:, count:] - 2.0 * border], axis=1)
    next_halo0 = [next_pay, from_next(behind(halo0[1], both))]
    there = from_next(here)
    cross = products(behind(odd, border), other, own + image)
    border = border_products(behind(odd, cross, there), border_kernel, own + other, halo0 + next_halo0)
    cross = jnp.concatenate([cross[:, :count], 2.0 * (cross[:, count:] - border)], axis=1)
    sums = partial_sums(jnp.concatenate([here, cross, there], axis=0), "gz")[-1]
    inverse, projected = factor(sums, scale)
    basis = basis_of(odd, own + other, inverse)
    return basis[None], projected[None]


def solution(mesh):
    in_specs = (
        P("cuts", None, "gz", None, None),
        P("gz", None, None),
        P("cuts"),
        P("cuts"),
        P("cuts", None),
    )
    out_specs = (P("cuts", None, "gz", None, None), P("cuts", None, None))
    return jax.shard_map(body, mesh=mesh, in_specs=in_specs, out_specs=out_specs, check_vma=False)
```

```python
import functools

import jax
import jax.numpy as jnp
from jax import lax
from jax.experimental import pallas as pl
from jax.experimental.pallas import tpu as pltpu
from jax.sharding import PartitionSpec as P

F32 = jnp.float32
GROUP = 8
ROWS = 8
SPAN = 64
VMEM = pl.BlockSpec(memory_space=pltpu.VMEM)
SMEM = pl.BlockSpec(memory_space=pltpu.SMEM)
PARAMS = pltpu.CompilerParams(vmem_limit_bytes=24 * 1024 * 1024)
ALONE = pltpu.CompilerParams(vmem_limit_bytes=56 * 1024 * 1024)

TERMS = ((2, 0), (1, 1), (0, 2), (1, 0), (0, 1), (0, 0))


def three_parts(value):
    parts = []
    for _ in range(3):
        parts.append(value.astype(jnp.bfloat16))
        value = value - parts[-1].astype(F32)
    return parts


def dot_wide(left, right):
    m, n = left.shape[0], right.shape[0]
    terms = lax.dot_general(
        jnp.concatenate(three_parts(left), axis=0),
        jnp.concatenate(three_parts(right), axis=0),
        (((1,), (1,)), ((), ())),
        preferred_element_type=F32,
    )
    return sum(terms[i * m : (i + 1) * m, j * n : (j + 1) * n] for i, j in TERMS)


def dot_tall(left, right):
    lefts, rights = three_parts(left), three_parts(right)
    return jnp.dot(
        jnp.concatenate([lefts[i] for i, _ in TERMS], axis=1),
        jnp.concatenate([rights[j] for _, j in TERMS], axis=0),
        preferred_element_type=F32,
    )


def dot_nt(left, right):
    return lax.dot_general(
        left, right, (((1,), (1,)), ((), ())), precision=lax.Precision.HIGHEST, preferred_element_type=F32
    )


def dot_nn(left, right):
    return jnp.dot(left, right, precision=lax.Precision.HIGHEST, preferred_element_type=F32)


def struct(*shape):
    return jax.ShapeDtypeStruct(shape, F32)


def cost(flops, nbytes):
    return pl.CostEstimate(flops=int(flops), bytes_accessed=int(nbytes), transcendentals=0)


SMALL = cost(1000, 1000)


def chunk_kernel(odd_ref, field0, field1, onsite_ref, out):
    size_x = field0.shape[2]
    for layer, source in enumerate((field0, field1)):
        flat = source.reshape(GROUP * size_x, source.shape[3])
        for j in range(size_x):
            out[layer * size_x + j] = flat[pl.ds(j, GROUP, stride=size_x), :]
    for j in range(out.shape[0] - 2 * size_x):
        out[2 * size_x + j] = onsite_ref[0, j * GROUP : (j + 1) * GROUP, :]


def to_chunk(field, onsite, odd, which):
    _, layers, size_x, size_y = field.shape
    rows = layers * size_x + (size_x // GROUP if which == 0 else 0)
    return pl.pallas_call(
        chunk_kernel,
        grid_spec=pltpu.PrefetchScalarGridSpec(
            num_scalar_prefetch=1,
            grid=(1,),
            in_specs=[
                pl.BlockSpec((GROUP, 1, size_x, size_y), lambda b, odd: (which, odd[0], 0, 0)),
                pl.BlockSpec((GROUP, 1, size_x, size_y), lambda b, odd: (which, 1 - odd[0], 0, 0)),
                pl.BlockSpec((1, size_x, size_y), lambda b, odd: (odd[0], 0, 0)),
            ],
            out_specs=pl.BlockSpec((rows, GROUP, size_y), lambda b, odd: (0, 0, 0)),
        ),
        out_shape=struct(rows, GROUP, size_y),
        compiler_params=ALONE if which == 0 else PARAMS,
        cost_estimate=SMALL,
        name="to_chunk",
    )(odd, field, field, onsite)


def beside_in_y(value):
    lane = lax.broadcasted_iota(jnp.int32, value.shape, 1)
    size = value.shape[1]
    left = jnp.where(lane > 0, pltpu.roll(value, 1, 1), 0.0)
    right = jnp.where(lane < size - 1, pltpu.roll(value, size - 1, 1), 0.0)
    return left + right


def beside(ref, x, first, last):
    size_x = ref.shape[0]
    low = ref[x - 1] if first is None else jnp.where(first, ref[jnp.maximum(x - 1, 0)], 0.0)
    high = ref[x + 1] if last is None else jnp.where(last, ref[jnp.minimum(x + 1, size_x - 1)], 0.0)
    return (low + high) + beside_in_y(ref[x])


def over_rows(size_x, step):
    blocks = size_x // ROWS

    def wrapped(block, _):
        for i in range(ROWS):
            first = block > 0 if i == 0 else None
            last = block < blocks - 1 if i == ROWS - 1 else None
            step(block * ROWS + i, first, last)
        return 0

    lax.fori_loop(0, blocks, wrapped, 0)


def layers_of(ref, size_x):
    return ref.at[pl.ds(0, size_x)], ref.at[pl.ds(size_x, size_x)]


def row_of(site, x):
    return site[pl.ds(x, 1), :]


def factors(center, inv_half, cheb):
    h = inv_half[0]
    return center[0], cheb[0, 0] - cheb[0, 2], cheb[0, 1] * h, 2.0 * cheb[0, 2] * h * h


def local_kernel(token, center, inv_half, cheb, own, near, ons, ons_near, out, once, inner):
    size_x = once.shape[0]
    middle, a, b, g = factors(center, inv_half, cheb)
    own0, own1 = layers_of(own, size_x)
    near0, near1 = layers_of(near, size_x)
    out0, out1 = layers_of(out, size_x)

    def layer(here, sides, beyond, site, side_sites, result):
        def first(x, top, end):
            around = sum(side[x] for side in sides)
            t = (row_of(site, x) - middle) * here[x] - beside(here, x, top, end) - around
            once[x] = t
            inner[x] = t - around

        def second(x, top, end):
            t = once[x]
            twice = (row_of(site, x) - middle) * t - beside(inner, x, top, end)
            for side, energies in zip(sides, side_sites):
                twice = twice - (row_of(energies, x) - middle) * side[x]
            twice = twice + 2.0 * here[x] + beyond[x]
            result[x] = a * here[x] + b * t + g * twice

        over_rows(size_x, first)
        over_rows(size_x, second)

    layer(own1, (own0, near1), near0, ons.at[1], (ons.at[0], ons_near), out1)
    layer(own0, (own1,), near1, ons.at[0], (ons.at[1],), out0)


def filter_local(token, scalars, own, near, ons, ons_near):
    _, size_x, size_y = ons.shape
    layer = pltpu.VMEM((size_x, GROUP, size_y), F32)
    return pl.pallas_call(
        local_kernel,
        in_specs=[SMEM] * 4 + [VMEM] * 4,
        out_specs=VMEM,
        out_shape=struct(2 * size_x, GROUP, size_y),
        scratch_shapes=[layer, layer],
        compiler_params=PARAMS,
        cost_estimate=SMALL,
        name="filter_local",
    )(token, *scalars, own, near, ons, ons_near)


def far_kernel(odd_ref, center, inv_half, cheb, base, far, ons, ons_far, out, pay):
    _, size_x, size_y = ons.shape
    middle, a, b, g = factors(center, inv_half, cheb)
    base0, base1 = layers_of(base, size_x)
    far0, far1 = layers_of(far, size_x)
    out0, out1 = layers_of(out, size_x)
    shift = b - 2.0 * g * middle

    def step(x, top, end):
        value = far0[x]
        site = g * (row_of(ons.at[0], x) + row_of(ons_far, x)) + shift
        out0[x] = base0[x] + ((2.0 * g) * beside(far0, x, top, end) - site * value + g * far1[x])
        out1[x] = base1[x] + g * value

    over_rows(size_x, step)
    half = size_x // 2
    start = (1 - odd_ref[0]) * half

    def copy(block, _):
        pay[pl.ds(block * ROWS, ROWS)] = out[pl.ds(start + block * ROWS, ROWS)]
        return 0

    lax.fori_loop(0, half // ROWS, copy, 0)


def filter_far(odd, scalars, base, far, ons, ons_far):
    _, size_x, size_y = ons.shape
    return pl.pallas_call(
        far_kernel,
        in_specs=[SMEM] * 4 + [VMEM] * 4,
        out_specs=[VMEM] * 2,
        out_shape=[struct(2 * size_x, GROUP, size_y), struct(size_x // 2, GROUP, size_y)],
        compiler_params=PARAMS,
        cost_estimate=SMALL,
        name="filter_far",
    )(odd, *scalars, base, far, ons, ons_far)


def image_kernel(token, own, beyond, ons, out):
    size_x = ons.shape[1]
    own0, own1 = layers_of(own, size_x)
    out0, out1 = layers_of(out, size_x)

    def step(x, top, end):
        value0, value1 = own0[x], own1[x]
        out0[x] = row_of(ons.at[0], x) * value0 - beside(own0, x, top, end) - value1
        out1[x] = row_of(ons.at[1], x) * value1 - beside(own1, x, top, end) - (value0 + beyond[size_x + x])

    over_rows(size_x, step)


def stage_kernel(token, center, inv_half, cheb, own, beyond, mine, near, ons, ons_near, image, base, once, inner):
    image_kernel(token, own, beyond, ons, image)
    local_kernel(token, center, inv_half, cheb, mine, near, ons, ons_near, base, once, inner)


def stage(token, scalars, own, beyond, mine, near, ons, ons_near):
    _, size_x, size_y = ons.shape
    layer = pltpu.VMEM((size_x, GROUP, size_y), F32)
    chunk = struct(2 * size_x, GROUP, size_y)
    return pl.pallas_call(
        stage_kernel,
        in_specs=[SMEM] * 4 + [VMEM] * 6,
        out_specs=[VMEM] * 2,
        out_shape=[chunk, chunk],
        scratch_shapes=[layer, layer],
        compiler_params=PARAMS,
        cost_estimate=SMALL,
        name="stage",
    )(token, *scalars, own, beyond, mine, near, ons, ons_near)


def image_chunk(token, own, beyond, ons):
    return pl.pallas_call(
        image_kernel,
        in_specs=[SMEM] + [VMEM] * 3,
        out_specs=VMEM,
        out_shape=struct(*own.shape),
        compiler_params=PARAMS,
        cost_estimate=SMALL,
        name="image_chunk",
    )(token, own, beyond, ons)


def wide(refs, x, rows):
    return jnp.concatenate([jnp.concatenate([ref[x + i] for i in range(rows)], axis=1) for ref in refs], axis=0)


def products_kernel(lefts, itself, token, *refs):
    left, right, out = refs[:lefts], refs[lefts:-1], refs[-1]
    rows = left[0].shape[0]

    @pl.when(pl.program_id(0) == 0)
    def _():
        out[...] = jnp.zeros_like(out)

    here, there = wide(left, 0, rows), wide(right, 0, rows)
    if itself:
        there = jnp.concatenate([here, there], axis=0)
    out[...] += dot_wide(here, there)


def products(token, left, right, itself=False):
    rows_all, _, size_y = left[0].shape
    part = pl.BlockSpec((SPAN, GROUP, size_y), lambda b, token: (b, 0, 0))
    columns = len(right) + (len(left) if itself else 0)
    shape = (len(left) * GROUP, columns * GROUP)
    return pl.pallas_call(
        functools.partial(products_kernel, len(left), itself),
        grid_spec=pltpu.PrefetchScalarGridSpec(
            num_scalar_prefetch=1,
            grid=(rows_all // SPAN,),
            in_specs=[part] * (len(left) + len(right)),
            out_specs=pl.BlockSpec(shape, lambda b, token: (0, 0)),
        ),
        out_shape=struct(*shape),
        compiler_params=PARAMS,
        cost_estimate=SMALL,
        name="products",
    )(token, *left, *right)


def border_kernel(count, odd_ref, *refs):
    own, other, halos, next_halos, out = refs[:count], refs[count : 2 * count], refs[-5:-3], refs[-3:-1], refs[-1]
    half = own[0].shape[0]

    def step(block, total):
        x = block * SPAN

        def beyond(stacks):
            return wide([stack.at[i] for stack in stacks for i in range(stack.shape[0])], x, SPAN)

        left = jnp.concatenate([wide(other, x, SPAN), beyond(next_halos)], axis=1)
        return total + dot_wide(left, jnp.concatenate([beyond(halos), wide(own, x, SPAN)], axis=1))

    out[...] = lax.fori_loop(0, half // SPAN, step, jnp.zeros(out.shape, F32))


def own_border_kernel(count, odd_ref, *refs):
    own, halos, out = refs[:count], refs[count:-1], refs[-1]
    half = own[0].shape[0]

    def step(block, total):
        x = block * SPAN
        there = wide([stack.at[i] for stack in halos for i in range(stack.shape[0])], x, SPAN)
        return total + dot_wide(wide(own, x, SPAN), there)

    out[...] = lax.fori_loop(0, half // SPAN, step, jnp.zeros(out.shape, F32))


def border_products(odd, kernel, layers, halos):
    _, half, _, size_y = halos[0].shape
    size = sum(stack.shape[0] for stack in halos[:2]) * GROUP
    mine = pl.BlockSpec((half, GROUP, size_y), lambda b, odd: (odd[0], 0, 0))
    theirs = [pl.BlockSpec(stack.shape, lambda b, odd: (0, 0, 0, 0)) for stack in halos]
    return pl.pallas_call(
        functools.partial(kernel, size // GROUP),
        grid_spec=pltpu.PrefetchScalarGridSpec(
            num_scalar_prefetch=1,
            grid=(1,),
            in_specs=[mine] * len(layers) + theirs,
            out_specs=pl.BlockSpec((size, size), lambda b, odd: (0, 0)),
        ),
        out_shape=struct(size, size),
        compiler_params=PARAMS,
        cost_estimate=SMALL,
        name="border_products",
    )(odd, *layers, *halos)


def inverse_factor(matrix):
    size = matrix.shape[0]
    row = lax.broadcasted_iota(jnp.int32, (size, size), 0)
    col = lax.broadcasted_iota(jnp.int32, (size, size), 1)
    identity = jnp.where(row == col, 1.0, 0.0)
    work = jnp.concatenate([matrix, identity], axis=1)
    below = lax.broadcasted_iota(jnp.int32, work.shape, 0)
    for j in range(0, size, GROUP):
        columns = [jnp.broadcast_to(work[:, j + k : j + k + 1], work.shape) for k in range(GROUP)]
        rows = [work[j + k : j + k + 1, :] for k in range(GROUP)]
        steps = []
        for k in range(GROUP):
            steps.append(rows[k] / columns[k][j + k : j + k + 1, :])
            for m in range(k + 1, GROUP):
                share = columns[k][j + m : j + m + 1, :]
                rows[m] = rows[m] - share * steps[k]
                columns[m] = columns[m] - columns[k] * (share / columns[k][j + k : j + k + 1, :])
        rest = work
        for k in range(GROUP):
            rest = rest - columns[k] * steps[k]
        for k in range(GROUP):
            rest = jnp.where(below == j + k, rows[k], rest)
        work = jnp.where(below < j, work, rest)
    pivots = jnp.sum(work[:, :size] * identity, axis=1, keepdims=True)
    return work[:, size:] / jnp.sqrt(pivots)


def with_shift(gram, scale):
    row = lax.broadcasted_iota(jnp.int32, gram.shape, 0)
    col = lax.broadcasted_iota(jnp.int32, gram.shape, 1)
    return gram * scale + jnp.where(row == col, 0.25, 0.0)


def factor_kernel(scale, sums, inverse_out, projected):
    size = sums.shape[0] // 3
    own, cross, other = (sums[i * size : (i + 1) * size, :] for i in range(3))
    top = inverse_factor(with_shift(own[:, :size], scale))
    low = dot_nt(cross[:, :size] * scale, top)
    inverse = inverse_factor(with_shift(other[:, :size], scale) - dot_nt(low, low))
    side = -dot_nn(inverse, dot_nn(low, top))
    whole = jnp.concatenate(
        [jnp.concatenate([top, jnp.zeros_like(top)], axis=1), jnp.concatenate([side, inverse], axis=1)], axis=0
    )
    inverse_out[...] = whole
    here, mixed, there = own[:, size:], cross[:, size:], other[:, size:]
    upper = jnp.concatenate([here + here.T, mixed.T], axis=1)
    lower = jnp.concatenate([mixed, there + there.T], axis=1)
    matrix = jnp.concatenate([upper, lower], axis=0) * (0.5 * scale)
    projected[...] = dot_nt(dot_nn(whole, matrix), whole)


def factor(sums, scale):
    size = sums.shape[0] // 3
    return pl.pallas_call(
        functools.partial(factor_kernel, scale),
        in_specs=[VMEM],
        out_specs=[VMEM] * 2,
        out_shape=[struct(2 * size, 2 * size)] * 2,
        compiler_params=PARAMS,
        cost_estimate=SMALL,
        name="factor",
    )(sums)


def basis_kernel(count, odd_ref, *refs):
    parts, coef, out = refs[:count], refs[count], refs[-1]
    rows, _, size_y = parts[0].shape
    result = dot_tall(coef[...], wide(parts, 0, rows))
    for v in range(0, out.shape[0], GROUP):
        for j in range(0, rows, GROUP):
            pieces = [result[v : v + GROUP, (j + i) * size_y : (j + i + 1) * size_y] for i in range(GROUP)]
            out[v : v + GROUP, 0, j : j + GROUP, :] = jnp.swapaxes(jnp.stack(pieces, axis=0), 0, 1)


def basis_of(odd, parts, coef):
    rows_all, _, size_y = parts[0].shape
    layers, rows = 2, SPAN
    size_x = rows_all // layers
    blocks = size_x // rows
    size = coef.shape[0]
    part = pl.BlockSpec((rows, GROUP, size_y), lambda s, b, odd: (s * blocks + b, 0, 0))
    return pl.pallas_call(
        functools.partial(basis_kernel, len(parts)),
        grid_spec=pltpu.PrefetchScalarGridSpec(
            num_scalar_prefetch=1,
            grid=(layers, blocks),
            in_specs=[part] * len(parts) + [pl.BlockSpec(coef.shape, lambda s, b, odd: (0, 0))],
            out_specs=pl.BlockSpec((size, 1, rows, size_y), lambda s, b, odd: (0, (s + odd[0]) % 2, b, 0)),
        ),
        out_shape=struct(size, layers, size_x, size_y),
        compiler_params=PARAMS,
        cost_estimate=SMALL,
        name="basis_of",
    )(odd, *parts, coef)


def behind(value, *others):
    return lax.optimization_barrier((value, *others))[0]


def partial_sums(value, axis, *others):
    size = lax.axis_size(axis)
    if size & (size - 1):
        return [lax.psum(value, axis)]
    sums = []
    step = 1
    while step < size:
        value = value + lax.ppermute(value, axis, [(i, i ^ step) for i in range(size)])
        if step == 1:
            value = behind(value, *others)
        sums.append(value)
        step *= 2
    return sums


def body(vectors, onsite, center, inv_half, cheb_coef):
    field = vectors[0]
    count, layers, size_x, size_y = field.shape
    ring = lax.axis_size("gz")
    cuts = lax.axis_size("cuts")
    scale = 1.0 / (layers * ring * size_x * size_y)
    odd = (lax.axis_index("gz") % 2).astype(jnp.int32)[None]
    across = [(i, (i + 1) % ring if i % 2 else (i - 1) % ring) for i in range(ring)]
    pair = [(i, i ^ 1) for i in range(ring)]
    left = [(i, i - 1) for i in range(1, cuts)]

    def inter_swap(value):
        return lax.ppermute(value, "gz", across)

    def intra_swap(value):
        return lax.ppermute(value, "gz", pair)

    def from_next(value):
        return lax.ppermute(value, "cuts", left)

    scalars = (center, inv_half, cheb_coef)
    ons = jnp.where(odd[0] == 0, onsite, onsite[::-1])
    groups = range(count // GROUP)

    mine, near, far = [], [], []
    token = odd
    for i in groups:
        mine.append(to_chunk(field, onsite, behind(odd, token), i))
        token = mine[-1]
    rows = layers * size_x
    near = [intra_swap(mine[0])]
    ons_near = intra_swap(ons[1])
    for i in groups[1:]:
        near.append(intra_swap(behind(mine[i], near[-1])))
    far = [inter_swap(mine[0]), inter_swap(behind(mine[1], near[0]))]

    def local(i, *tokens):
        return filter_local(behind(odd, *tokens), scalars, mine[i], near[i], ons, ons_near)

    base = local(0, mine[-1])
    far[0] = behind(far[0], base)
    ons_far = far[0][rows:].reshape(size_x, size_y)
    own, other, image, pay, beyond = [], [], [], [], []
    last = len(groups) - 1
    for i in groups:
        out, half = filter_far(behind(odd, base), scalars, base, far[i], ons, ons_far)
        own.append(out)
        pay.append(half)
        other.append(from_next(out))
        beyond.append(intra_swap(out))
        if i + 2 <= last:
            far.append(inter_swap(behind(mine[i + 2], far[i])))
        token = behind(odd, out, *other[i - 1 : i]) if i else behind(odd, out)
        if i == 0:
            base = local(1, token)
        elif i < last:
            done, base = stage(token, scalars, own[i - 1], beyond[i - 1], mine[i + 1], near[i + 1], ons, ons_near)
            image.append(done)
        else:
            image.append(image_chunk(token, own[i - 1], beyond[i - 1], ons))
            image.append(image_chunk(behind(odd, image[-1]), own[i], beyond[i], ons))

    middle = (last + 1) // 2
    halo0 = [inter_swap(behind(jnp.stack(pay[:middle]), own[-1])), inter_swap(jnp.stack(pay[middle:]))]
    both = products(odd, own, image, True)
    start = (1 - odd[0]) * (size_x // 2)
    next_pay = [lax.dynamic_slice_in_dim(behind(value, both), start, size_x // 2, 0) for value in other[:middle]]
    next_pay = inter_swap(jnp.stack(next_pay))
    border = border_products(behind(odd, both), own_border_kernel, own, halo0)
    here = jnp.concatenate([both[:, :count], both[:, count:] - 2.0 * border], axis=1)
    next_halo0 = [next_pay, from_next(behind(halo0[1], both))]
    there = from_next(here)
    cross = products(behind(odd, border), other, own + image)
    border = border_products(behind(odd, cross, there), border_kernel, own + other, halo0 + next_halo0)
    cross = jnp.concatenate([cross[:, :count], 2.0 * (cross[:, count:] - border)], axis=1)
    sums = partial_sums(jnp.concatenate([here, cross, there], axis=0), "gz")[-1]
    inverse, projected = factor(sums, scale)
    basis = basis_of(odd, own + other, inverse)
    return basis[None], projected[None]


def solution(mesh):
    in_specs = (
        P("cuts", None, "gz", None, None),
        P("gz", None, None),
        P("cuts"),
        P("cuts"),
        P("cuts", None),
    )
    out_specs = (P("cuts", None, "gz", None, None), P("cuts", None, None))
    return jax.shard_map(body, mesh=mesh, in_specs=in_specs, out_specs=out_specs, check_vma=False)
```

```python
import functools

import jax
import jax.numpy as jnp
from jax import lax
from jax.experimental import pallas as pl
from jax.experimental.pallas import tpu as pltpu
from jax.sharding import PartitionSpec as P

F32 = jnp.float32
GROUP = 8
ROWS = 8
SPAN = 64
VMEM = pl.BlockSpec(memory_space=pltpu.VMEM)
SMEM = pl.BlockSpec(memory_space=pltpu.SMEM)
PARAMS = pltpu.CompilerParams(vmem_limit_bytes=24 * 1024 * 1024)
ALONE = pltpu.CompilerParams(vmem_limit_bytes=56 * 1024 * 1024)

TERMS = ((2, 0), (1, 1), (0, 2), (1, 0), (0, 1), (0, 0))


def three_parts(value):
    parts = []
    for _ in range(3):
        parts.append(value.astype(jnp.bfloat16))
        value = value - parts[-1].astype(F32)
    return parts


def dot_wide(left, right):
    m, n = left.shape[0], right.shape[0]
    terms = lax.dot_general(
        jnp.concatenate(three_parts(left), axis=0),
        jnp.concatenate(three_parts(right), axis=0),
        (((1,), (1,)), ((), ())),
        preferred_element_type=F32,
    )
    return sum(terms[i * m : (i + 1) * m, j * n : (j + 1) * n] for i, j in TERMS)


def dot_tall(left, right):
    lefts, rights = three_parts(left), three_parts(right)
    return jnp.dot(
        jnp.concatenate([lefts[i] for i, _ in TERMS], axis=1),
        jnp.concatenate([rights[j] for _, j in TERMS], axis=0),
        preferred_element_type=F32,
    )


def dot_nt(left, right):
    return lax.dot_general(
        left, right, (((1,), (1,)), ((), ())), precision=lax.Precision.HIGHEST, preferred_element_type=F32
    )


def dot_nn(left, right):
    return jnp.dot(left, right, precision=lax.Precision.HIGHEST, preferred_element_type=F32)


def struct(*shape):
    return jax.ShapeDtypeStruct(shape, F32)


def cost(flops, nbytes):
    return pl.CostEstimate(flops=int(flops), bytes_accessed=int(nbytes), transcendentals=0)


SMALL = cost(1000, 1000)


def chunk_kernel(odd_ref, field0, field1, onsite_ref, out):
    size_x = field0.shape[2]
    for layer, source in enumerate((field0, field1)):
        for j in range(0, size_x, GROUP):
            here = pl.ds(layer * size_x + j, GROUP)
            out[here] = jnp.swapaxes(source[:, 0, j : j + GROUP, :], 0, 1)
    for j in range(out.shape[0] - 2 * size_x):
        out[2 * size_x + j] = onsite_ref[0, j * GROUP : (j + 1) * GROUP, :]


def to_chunk(field, onsite, odd, which):
    _, layers, size_x, size_y = field.shape
    rows = layers * size_x + (size_x // GROUP if which == 0 else 0)
    return pl.pallas_call(
        chunk_kernel,
        grid_spec=pltpu.PrefetchScalarGridSpec(
            num_scalar_prefetch=1,
            grid=(1,),
            in_specs=[
                pl.BlockSpec((GROUP, 1, size_x, size_y), lambda b, odd: (which, odd[0], 0, 0)),
                pl.BlockSpec((GROUP, 1, size_x, size_y), lambda b, odd: (which, 1 - odd[0], 0, 0)),
                pl.BlockSpec((1, size_x, size_y), lambda b, odd: (odd[0], 0, 0)),
            ],
            out_specs=pl.BlockSpec((rows, GROUP, size_y), lambda b, odd: (0, 0, 0)),
        ),
        out_shape=struct(rows, GROUP, size_y),
        compiler_params=ALONE if which == 0 else PARAMS,
        cost_estimate=SMALL,
        name="to_chunk",
    )(odd, field, field, onsite)


def beside_in_y(value):
    lane = lax.broadcasted_iota(jnp.int32, value.shape, 1)
    size = value.shape[1]
    left = jnp.where(lane > 0, pltpu.roll(value, 1, 1), 0.0)
    right = jnp.where(lane < size - 1, pltpu.roll(value, size - 1, 1), 0.0)
    return left + right


def beside(ref, x, first, last):
    size_x = ref.shape[0]
    low = ref[x - 1] if first is None else jnp.where(first, ref[jnp.maximum(x - 1, 0)], 0.0)
    high = ref[x + 1] if last is None else jnp.where(last, ref[jnp.minimum(x + 1, size_x - 1)], 0.0)
    return (low + high) + beside_in_y(ref[x])


def over_rows(size_x, step):
    blocks = size_x // ROWS

    def wrapped(block, _):
        for i in range(ROWS):
            first = block > 0 if i == 0 else None
            last = block < blocks - 1 if i == ROWS - 1 else None
            step(block * ROWS + i, first, last)
        return 0

    lax.fori_loop(0, blocks, wrapped, 0)


def layers_of(ref, size_x):
    return ref.at[pl.ds(0, size_x)], ref.at[pl.ds(size_x, size_x)]


def row_of(site, x):
    return site[pl.ds(x, 1), :]


def factors(center, inv_half, cheb):
    h = inv_half[0]
    return center[0], cheb[0, 0] - cheb[0, 2], cheb[0, 1] * h, 2.0 * cheb[0, 2] * h * h


def local_kernel(token, center, inv_half, cheb, own, near, ons, ons_near, out, once, inner):
    size_x = once.shape[0]
    middle, a, b, g = factors(center, inv_half, cheb)
    own0, own1 = layers_of(own, size_x)
    near0, near1 = layers_of(near, size_x)
    out0, out1 = layers_of(out, size_x)

    def layer(here, sides, beyond, site, side_sites, result):
        def first(x, top, end):
            around = sum(side[x] for side in sides)
            t = (row_of(site, x) - middle) * here[x] - beside(here, x, top, end) - around
            once[x] = t
            inner[x] = t - around

        def second(x, top, end):
            t = once[x]
            twice = (row_of(site, x) - middle) * t - beside(inner, x, top, end)
            for side, energies in zip(sides, side_sites):
                twice = twice - (row_of(energies, x) - middle) * side[x]
            twice = twice + 2.0 * here[x] + beyond[x]
            result[x] = a * here[x] + b * t + g * twice

        over_rows(size_x, first)
        over_rows(size_x, second)

    layer(own1, (own0, near1), near0, ons.at[1], (ons.at[0], ons_near), out1)
    layer(own0, (own1,), near1, ons.at[0], (ons.at[1],), out0)


def filter_local(token, scalars, own, near, ons, ons_near):
    _, size_x, size_y = ons.shape
    layer = pltpu.VMEM((size_x, GROUP, size_y), F32)
    return pl.pallas_call(
        local_kernel,
        in_specs=[SMEM] * 4 + [VMEM] * 4,
        out_specs=VMEM,
        out_shape=struct(2 * size_x, GROUP, size_y),
        scratch_shapes=[layer, layer],
        compiler_params=PARAMS,
        cost_estimate=SMALL,
        name="filter_local",
    )(token, *scalars, own, near, ons, ons_near)


def far_kernel(odd_ref, center, inv_half, cheb, base, far, ons, ons_far, out, pay):
    _, size_x, size_y = ons.shape
    middle, a, b, g = factors(center, inv_half, cheb)
    base0, base1 = layers_of(base, size_x)
    far0, far1 = layers_of(far, size_x)
    out0, out1 = layers_of(out, size_x)
    shift = b - 2.0 * g * middle

    def step(x, top, end):
        value = far0[x]
        site = g * (row_of(ons.at[0], x) + row_of(ons_far, x)) + shift
        out0[x] = base0[x] + ((2.0 * g) * beside(far0, x, top, end) - site * value + g * far1[x])
        out1[x] = base1[x] + g * value

    over_rows(size_x, step)
    half = size_x // 2
    start = (1 - odd_ref[0]) * half

    def copy(block, _):
        pay[pl.ds(block * ROWS, ROWS)] = out[pl.ds(start + block * ROWS, ROWS)]
        return 0

    lax.fori_loop(0, half // ROWS, copy, 0)


def filter_far(odd, scalars, base, far, ons, ons_far):
    _, size_x, size_y = ons.shape
    return pl.pallas_call(
        far_kernel,
        in_specs=[SMEM] * 4 + [VMEM] * 4,
        out_specs=[VMEM] * 2,
        out_shape=[struct(2 * size_x, GROUP, size_y), struct(size_x // 2, GROUP, size_y)],
        compiler_params=PARAMS,
        cost_estimate=SMALL,
        name="filter_far",
    )(odd, *scalars, base, far, ons, ons_far)


def image_kernel(token, own, beyond, ons, out):
    size_x = ons.shape[1]
    own0, own1 = layers_of(own, size_x)
    out0, out1 = layers_of(out, size_x)

    def step(x, top, end):
        value0, value1 = own0[x], own1[x]
        out0[x] = row_of(ons.at[0], x) * value0 - beside(own0, x, top, end) - value1
        out1[x] = row_of(ons.at[1], x) * value1 - beside(own1, x, top, end) - (value0 + beyond[size_x + x])

    over_rows(size_x, step)


def stage_kernel(token, center, inv_half, cheb, own, beyond, mine, near, ons, ons_near, image, base, once, inner):
    image_kernel(token, own, beyond, ons, image)
    local_kernel(token, center, inv_half, cheb, mine, near, ons, ons_near, base, once, inner)


def stage(token, scalars, own, beyond, mine, near, ons, ons_near):
    _, size_x, size_y = ons.shape
    layer = pltpu.VMEM((size_x, GROUP, size_y), F32)
    chunk = struct(2 * size_x, GROUP, size_y)
    return pl.pallas_call(
        stage_kernel,
        in_specs=[SMEM] * 4 + [VMEM] * 6,
        out_specs=[VMEM] * 2,
        out_shape=[chunk, chunk],
        scratch_shapes=[layer, layer],
        compiler_params=PARAMS,
        cost_estimate=SMALL,
        name="stage",
    )(token, *scalars, own, beyond, mine, near, ons, ons_near)


def image_chunk(token, own, beyond, ons):
    return pl.pallas_call(
        image_kernel,
        in_specs=[SMEM] + [VMEM] * 3,
        out_specs=VMEM,
        out_shape=struct(*own.shape),
        compiler_params=PARAMS,
        cost_estimate=SMALL,
        name="image_chunk",
    )(token, own, beyond, ons)


def wide(refs, x, rows):
    return jnp.concatenate([jnp.concatenate([ref[x + i] for i in range(rows)], axis=1) for ref in refs], axis=0)


def products_kernel(lefts, itself, token, *refs):
    left, right, out = refs[:lefts], refs[lefts:-1], refs[-1]
    rows = left[0].shape[0]

    @pl.when(pl.program_id(0) == 0)
    def _():
        out[...] = jnp.zeros_like(out)

    here, there = wide(left, 0, rows), wide(right, 0, rows)
    if itself:
        there = jnp.concatenate([here, there], axis=0)
    out[...] += dot_wide(here, there)


def products(token, left, right, itself=False):
    rows_all, _, size_y = left[0].shape
    part = pl.BlockSpec((SPAN, GROUP, size_y), lambda b, token: (b, 0, 0))
    columns = len(right) + (len(left) if itself else 0)
    shape = (len(left) * GROUP, columns * GROUP)
    return pl.pallas_call(
        functools.partial(products_kernel, len(left), itself),
        grid_spec=pltpu.PrefetchScalarGridSpec(
            num_scalar_prefetch=1,
            grid=(rows_all // SPAN,),
            in_specs=[part] * (len(left) + len(right)),
            out_specs=pl.BlockSpec(shape, lambda b, token: (0, 0)),
        ),
        out_shape=struct(*shape),
        compiler_params=PARAMS,
        cost_estimate=SMALL,
        name="products",
    )(token, *left, *right)


def border_kernel(count, odd_ref, *refs):
    own, other, halos, next_halos, out = refs[:count], refs[count : 2 * count], refs[-5:-3], refs[-3:-1], refs[-1]
    half = own[0].shape[0]

    def step(block, total):
        x = block * SPAN

        def beyond(stacks):
            return wide([stack.at[i] for stack in stacks for i in range(stack.shape[0])], x, SPAN)

        left = jnp.concatenate([wide(other, x, SPAN), beyond(next_halos)], axis=1)
        return total + dot_wide(left, jnp.concatenate([beyond(halos), wide(own, x, SPAN)], axis=1))

    out[...] = lax.fori_loop(0, half // SPAN, step, jnp.zeros(out.shape, F32))


def own_border_kernel(count, odd_ref, *refs):
    own, halos, out = refs[:count], refs[count:-1], refs[-1]
    half = own[0].shape[0]

    def step(block, total):
        x = block * SPAN
        there = wide([stack.at[i] for stack in halos for i in range(stack.shape[0])], x, SPAN)
        return total + dot_wide(wide(own, x, SPAN), there)

    out[...] = lax.fori_loop(0, half // SPAN, step, jnp.zeros(out.shape, F32))


def border_products(odd, kernel, layers, halos):
    _, half, _, size_y = halos[0].shape
    size = sum(stack.shape[0] for stack in halos[:2]) * GROUP
    mine = pl.BlockSpec((half, GROUP, size_y), lambda b, odd: (odd[0], 0, 0))
    theirs = [pl.BlockSpec(stack.shape, lambda b, odd: (0, 0, 0, 0)) for stack in halos]
    return pl.pallas_call(
        functools.partial(kernel, size // GROUP),
        grid_spec=pltpu.PrefetchScalarGridSpec(
            num_scalar_prefetch=1,
            grid=(1,),
            in_specs=[mine] * len(layers) + theirs,
            out_specs=pl.BlockSpec((size, size), lambda b, odd: (0, 0)),
        ),
        out_shape=struct(size, size),
        compiler_params=PARAMS,
        cost_estimate=SMALL,
        name="border_products",
    )(odd, *layers, *halos)


def inverse_factor(matrix):
    size = matrix.shape[0]
    row = lax.broadcasted_iota(jnp.int32, (size, size), 0)
    col = lax.broadcasted_iota(jnp.int32, (size, size), 1)
    identity = jnp.where(row == col, 1.0, 0.0)
    work = jnp.concatenate([matrix, identity], axis=1)
    below = lax.broadcasted_iota(jnp.int32, work.shape, 0)
    for j in range(0, size, GROUP):
        columns = [jnp.broadcast_to(work[:, j + k : j + k + 1], work.shape) for k in range(GROUP)]
        rows = [work[j + k : j + k + 1, :] for k in range(GROUP)]
        steps = []
        for k in range(GROUP):
            steps.append(rows[k] / columns[k][j + k : j + k + 1, :])
            for m in range(k + 1, GROUP):
                share = columns[k][j + m : j + m + 1, :]
                rows[m] = rows[m] - share * steps[k]
                columns[m] = columns[m] - columns[k] * (share / columns[k][j + k : j + k + 1, :])
        rest = work
        for k in range(GROUP):
            rest = rest - columns[k] * steps[k]
        for k in range(GROUP):
            rest = jnp.where(below == j + k, rows[k], rest)
        work = jnp.where(below < j, work, rest)
    pivots = jnp.sum(work[:, :size] * identity, axis=1, keepdims=True)
    return work[:, size:] / jnp.sqrt(pivots)


def with_shift(gram, scale):
    row = lax.broadcasted_iota(jnp.int32, gram.shape, 0)
    col = lax.broadcasted_iota(jnp.int32, gram.shape, 1)
    return gram * scale + jnp.where(row == col, 0.25, 0.0)


def factor_kernel(scale, sums, inverse_out, projected):
    size = sums.shape[0] // 3
    own, cross, other = (sums[i * size : (i + 1) * size, :] for i in range(3))
    top = inverse_factor(with_shift(own[:, :size], scale))
    low = dot_nt(cross[:, :size] * scale, top)
    inverse = inverse_factor(with_shift(other[:, :size], scale) - dot_nt(low, low))
    side = -dot_nn(inverse, dot_nn(low, top))
    whole = jnp.concatenate(
        [jnp.concatenate([top, jnp.zeros_like(top)], axis=1), jnp.concatenate([side, inverse], axis=1)], axis=0
    )
    inverse_out[...] = whole
    here, mixed, there = own[:, size:], cross[:, size:], other[:, size:]
    upper = jnp.concatenate([here + here.T, mixed.T], axis=1)
    lower = jnp.concatenate([mixed, there + there.T], axis=1)
    matrix = jnp.concatenate([upper, lower], axis=0) * (0.5 * scale)
    projected[...] = dot_nt(dot_nn(whole, matrix), whole)


def factor(sums, scale):
    size = sums.shape[0] // 3
    return pl.pallas_call(
        functools.partial(factor_kernel, scale),
        in_specs=[VMEM],
        out_specs=[VMEM] * 2,
        out_shape=[struct(2 * size, 2 * size)] * 2,
        compiler_params=PARAMS,
        cost_estimate=SMALL,
        name="factor",
    )(sums)


def basis_kernel(count, odd_ref, *refs):
    parts, coef, out = refs[:count], refs[count], refs[-1]
    rows, _, size_y = parts[0].shape
    result = dot_tall(coef[...], wide(parts, 0, rows))
    for v in range(0, out.shape[0], GROUP):
        for j in range(0, rows, GROUP):
            pieces = [result[v : v + GROUP, (j + i) * size_y : (j + i + 1) * size_y] for i in range(GROUP)]
            out[v : v + GROUP, 0, j : j + GROUP, :] = jnp.swapaxes(jnp.stack(pieces, axis=0), 0, 1)


def basis_of(odd, parts, coef):
    rows_all, _, size_y = parts[0].shape
    layers, rows = 2, SPAN
    size_x = rows_all // layers
    blocks = size_x // rows
    size = coef.shape[0]
    part = pl.BlockSpec((rows, GROUP, size_y), lambda s, b, odd: (s * blocks + b, 0, 0))
    return pl.pallas_call(
        functools.partial(basis_kernel, len(parts)),
        grid_spec=pltpu.PrefetchScalarGridSpec(
            num_scalar_prefetch=1,
            grid=(layers, blocks),
            in_specs=[part] * len(parts) + [pl.BlockSpec(coef.shape, lambda s, b, odd: (0, 0))],
            out_specs=pl.BlockSpec((size, 1, rows, size_y), lambda s, b, odd: (0, (s + odd[0]) % 2, b, 0)),
        ),
        out_shape=struct(size, layers, size_x, size_y),
        compiler_params=PARAMS,
        cost_estimate=SMALL,
        name="basis_of",
    )(odd, *parts, coef)


def behind(value, *others):
    return lax.optimization_barrier((value, *others))[0]


def partial_sums(value, axis, *others):
    size = lax.axis_size(axis)
    if size & (size - 1):
        return [lax.psum(value, axis)]
    sums = []
    step = 1
    while step < size:
        value = value + lax.ppermute(value, axis, [(i, i ^ step) for i in range(size)])
        if step == 1:
            value = behind(value, *others)
        sums.append(value)
        step *= 2
    return sums


def body(vectors, onsite, center, inv_half, cheb_coef):
    field = vectors[0]
    count, layers, size_x, size_y = field.shape
    ring = lax.axis_size("gz")
    cuts = lax.axis_size("cuts")
    scale = 1.0 / (layers * ring * size_x * size_y)
    odd = (lax.axis_index("gz") % 2).astype(jnp.int32)[None]
    across = [(i, (i + 1) % ring if i % 2 else (i - 1) % ring) for i in range(ring)]
    pair = [(i, i ^ 1) for i in range(ring)]
    left = [(i, i - 1) for i in range(1, cuts)]

    def inter_swap(value):
        return lax.ppermute(value, "gz", across)

    def intra_swap(value):
        return lax.ppermute(value, "gz", pair)

    def from_next(value):
        return lax.ppermute(value, "cuts", left)

    scalars = (center, inv_half, cheb_coef)
    ons = jnp.where(odd[0] == 0, onsite, onsite[::-1])
    groups = range(count // GROUP)

    mine, near, far = [], [], []
    token = odd
    for i in groups:
        mine.append(to_chunk(field, onsite, behind(odd, token), i))
        token = mine[-1]
    rows = layers * size_x
    near = [intra_swap(mine[0])]
    ons_near = intra_swap(ons[1])
    for i in groups[1:]:
        near.append(intra_swap(behind(mine[i], near[-1])))
    far = [inter_swap(mine[0]), inter_swap(behind(mine[1], near[0]))]

    def local(i, *tokens):
        return filter_local(behind(odd, *tokens), scalars, mine[i], near[i], ons, ons_near)

    base = local(0, mine[-1])
    far[0] = behind(far[0], base)
    ons_far = far[0][rows:].reshape(size_x, size_y)
    own, other, image, pay, beyond = [], [], [], [], []
    last = len(groups) - 1
    for i in groups:
        out, half = filter_far(behind(odd, base), scalars, base, far[i], ons, ons_far)
        own.append(out)
        pay.append(half)
        other.append(from_next(out))
        beyond.append(intra_swap(out))
        if i + 2 <= last:
            far.append(inter_swap(behind(mine[i + 2], far[i])))
        token = behind(odd, out, *other[i - 1 : i]) if i else behind(odd, out)
        if i == 0:
            base = local(1, token)
        elif i < last:
            done, base = stage(token, scalars, own[i - 1], beyond[i - 1], mine[i + 1], near[i + 1], ons, ons_near)
            image.append(done)
        else:
            image.append(image_chunk(token, own[i - 1], beyond[i - 1], ons))
            image.append(image_chunk(behind(odd, image[-1]), own[i], beyond[i], ons))

    middle = (last + 1) // 2
    halo0 = [inter_swap(behind(jnp.stack(pay[:middle]), own[-1])), inter_swap(jnp.stack(pay[middle:]))]
    both = products(odd, own, image, True)
    start = (1 - odd[0]) * (size_x // 2)
    next_pay = [lax.dynamic_slice_in_dim(behind(value, both), start, size_x // 2, 0) for value in other[:middle]]
    next_pay = inter_swap(jnp.stack(next_pay))
    border = border_products(behind(odd, both), own_border_kernel, own, halo0)
    here = jnp.concatenate([both[:, :count], both[:, count:] - 2.0 * border], axis=1)
    next_halo0 = [next_pay, from_next(behind(halo0[1], both))]
    there = from_next(here)
    cross = products(behind(odd, border), other, own + image)
    border = border_products(behind(odd, cross, there), border_kernel, own + other, halo0 + next_halo0)
    cross = jnp.concatenate([cross[:, :count], 2.0 * (cross[:, count:] - border)], axis=1)
    sums = partial_sums(jnp.concatenate([here, cross, there], axis=0), "gz")[-1]
    inverse, projected = factor(sums, scale)
    basis = basis_of(odd, own + other, inverse)
    return basis[None], projected[None]


def solution(mesh):
    in_specs = (
        P("cuts", None, "gz", None, None),
        P("gz", None, None),
        P("cuts"),
        P("cuts"),
        P("cuts", None),
    )
    out_specs = (P("cuts", None, "gz", None, None), P("cuts", None, None))
    return jax.shard_map(body, mesh=mesh, in_specs=in_specs, out_specs=out_specs, check_vma=False)
```

```python
import functools

import jax
import jax.numpy as jnp
from jax import lax
from jax.experimental import pallas as pl
from jax.experimental.pallas import tpu as pltpu
from jax.sharding import PartitionSpec as P

F32 = jnp.float32
GROUP = 8
ROWS = 8
SPAN = 64
VMEM = pl.BlockSpec(memory_space=pltpu.VMEM)
SMEM = pl.BlockSpec(memory_space=pltpu.SMEM)
PARAMS = pltpu.CompilerParams(vmem_limit_bytes=24 * 1024 * 1024)
ALONE = pltpu.CompilerParams(vmem_limit_bytes=56 * 1024 * 1024)

TERMS = ((2, 0), (1, 1), (0, 2), (1, 0), (0, 1), (0, 0))


def three_parts(value):
    parts = []
    for _ in range(3):
        parts.append(value.astype(jnp.bfloat16))
        value = value - parts[-1].astype(F32)
    return parts


def dot_wide(left, right):
    m, n = left.shape[0], right.shape[0]
    terms = lax.dot_general(
        jnp.concatenate(three_parts(left), axis=0),
        jnp.concatenate(three_parts(right), axis=0),
        (((1,), (1,)), ((), ())),
        preferred_element_type=F32,
    )
    return sum(terms[i * m : (i + 1) * m, j * n : (j + 1) * n] for i, j in TERMS)


def dot_tall(left, right):
    lefts, rights = three_parts(left), three_parts(right)
    return jnp.dot(
        jnp.concatenate([lefts[i] for i, _ in TERMS], axis=1),
        jnp.concatenate([rights[j] for _, j in TERMS], axis=0),
        preferred_element_type=F32,
    )


def dot_nt(left, right):
    return lax.dot_general(
        left, right, (((1,), (1,)), ((), ())), precision=lax.Precision.HIGHEST, preferred_element_type=F32
    )


def dot_nn(left, right):
    return jnp.dot(left, right, precision=lax.Precision.HIGHEST, preferred_element_type=F32)


def struct(*shape):
    return jax.ShapeDtypeStruct(shape, F32)


def cost(flops, nbytes):
    return pl.CostEstimate(flops=int(flops), bytes_accessed=int(nbytes), transcendentals=0)


SMALL = cost(1000, 1000)


def chunk_kernel(odd_ref, field0, field1, onsite_ref, out):
    size_x = field0.shape[2]
    for layer, source in enumerate((field0, field1)):
        for j in range(0, size_x, GROUP):
            here = pl.ds(layer * size_x + j, GROUP)
            out[here] = jnp.swapaxes(source[:, 0, j : j + GROUP, :], 0, 1)
    for j in range(out.shape[0] - 2 * size_x):
        out[2 * size_x + j] = onsite_ref[0, j * GROUP : (j + 1) * GROUP, :]


def to_chunk(field, onsite, odd, which):
    _, layers, size_x, size_y = field.shape
    rows = layers * size_x + (size_x // GROUP if which == 0 else 0)
    return pl.pallas_call(
        chunk_kernel,
        grid_spec=pltpu.PrefetchScalarGridSpec(
            num_scalar_prefetch=1,
            grid=(1,),
            in_specs=[
                pl.BlockSpec((GROUP, 1, size_x, size_y), lambda b, odd: (which, odd[0], 0, 0)),
                pl.BlockSpec((GROUP, 1, size_x, size_y), lambda b, odd: (which, 1 - odd[0], 0, 0)),
                pl.BlockSpec((1, size_x, size_y), lambda b, odd: (odd[0], 0, 0)),
            ],
            out_specs=pl.BlockSpec((rows, GROUP, size_y), lambda b, odd: (0, 0, 0)),
        ),
        out_shape=struct(rows, GROUP, size_y),
        compiler_params=ALONE if which == 0 else PARAMS,
        cost_estimate=SMALL,
        name="to_chunk",
    )(odd, field, field, onsite)


def beside_in_y(value):
    lane = lax.broadcasted_iota(jnp.int32, value.shape, 1)
    size = value.shape[1]
    left = jnp.where(lane > 0, pltpu.roll(value, 1, 1), 0.0)
    right = jnp.where(lane < size - 1, pltpu.roll(value, size - 1, 1), 0.0)
    return left + right


def beside(ref, x, first, last):
    size_x = ref.shape[0]
    low = ref[x - 1] if first is None else jnp.where(first, ref[jnp.maximum(x - 1, 0)], 0.0)
    high = ref[x + 1] if last is None else jnp.where(last, ref[jnp.minimum(x + 1, size_x - 1)], 0.0)
    return (low + high) + beside_in_y(ref[x])


def over_rows(size_x, step):
    blocks = size_x // ROWS

    def wrapped(block, _):
        for i in range(ROWS):
            first = block > 0 if i == 0 else None
            last = block < blocks - 1 if i == ROWS - 1 else None
            step(block * ROWS + i, first, last)
        return 0

    lax.fori_loop(0, blocks, wrapped, 0)


def layers_of(ref, size_x):
    return ref.at[pl.ds(0, size_x)], ref.at[pl.ds(size_x, size_x)]


def row_of(site, x):
    return site[pl.ds(x, 1), :]


def factors(center, inv_half, cheb):
    h = inv_half[0]
    return center[0], cheb[0, 0] - cheb[0, 2], cheb[0, 1] * h, 2.0 * cheb[0, 2] * h * h


def local_kernel(token, center, inv_half, cheb, own, near, ons, ons_near, out, once, inner):
    size_x = once.shape[0]
    middle, a, b, g = factors(center, inv_half, cheb)
    own0, own1 = layers_of(own, size_x)
    near0, near1 = layers_of(near, size_x)
    out0, out1 = layers_of(out, size_x)

    def layer(here, sides, beyond, site, side_sites, result):
        def first(x, top, end):
            around = sum(side[x] for side in sides)
            t = (row_of(site, x) - middle) * here[x] - beside(here, x, top, end) - around
            once[x] = t
            inner[x] = t - around

        def second(x, top, end):
            t = once[x]
            twice = (row_of(site, x) - middle) * t - beside(inner, x, top, end)
            for side, energies in zip(sides, side_sites):
                twice = twice - (row_of(energies, x) - middle) * side[x]
            twice = twice + 2.0 * here[x] + beyond[x]
            result[x] = a * here[x] + b * t + g * twice

        over_rows(size_x, first)
        over_rows(size_x, second)

    layer(own1, (own0, near1), near0, ons.at[1], (ons.at[0], ons_near), out1)
    layer(own0, (own1,), near1, ons.at[0], (ons.at[1],), out0)


def filter_local(token, scalars, own, near, ons, ons_near):
    _, size_x, size_y = ons.shape
    layer = pltpu.VMEM((size_x, GROUP, size_y), F32)
    return pl.pallas_call(
        local_kernel,
        in_specs=[SMEM] * 4 + [VMEM] * 4,
        out_specs=VMEM,
        out_shape=struct(2 * size_x, GROUP, size_y),
        scratch_shapes=[layer, layer],
        compiler_params=PARAMS,
        cost_estimate=SMALL,
        name="filter_local",
    )(token, *scalars, own, near, ons, ons_near)


def far_kernel(odd_ref, center, inv_half, cheb, base, far, ons, ons_far, out, pay):
    _, size_x, size_y = ons.shape
    middle, a, b, g = factors(center, inv_half, cheb)
    base0, base1 = layers_of(base, size_x)
    far0, far1 = layers_of(far, size_x)
    out0, out1 = layers_of(out, size_x)
    shift = b - 2.0 * g * middle

    def step(x, top, end):
        value = far0[x]
        site = g * (row_of(ons.at[0], x) + row_of(ons_far, x)) + shift
        out0[x] = base0[x] + ((2.0 * g) * beside(far0, x, top, end) - site * value + g * far1[x])
        out1[x] = base1[x] + g * value

    over_rows(size_x, step)
    half = size_x // 2
    start = (1 - odd_ref[0]) * half

    def copy(block, _):
        pay[pl.ds(block * ROWS, ROWS)] = out[pl.ds(start + block * ROWS, ROWS)]
        return 0

    lax.fori_loop(0, half // ROWS, copy, 0)


def filter_far(odd, scalars, base, far, ons, ons_far):
    _, size_x, size_y = ons.shape
    return pl.pallas_call(
        far_kernel,
        in_specs=[SMEM] * 4 + [VMEM] * 4,
        out_specs=[VMEM] * 2,
        out_shape=[struct(2 * size_x, GROUP, size_y), struct(size_x // 2, GROUP, size_y)],
        compiler_params=PARAMS,
        cost_estimate=SMALL,
        name="filter_far",
    )(odd, *scalars, base, far, ons, ons_far)


def image_kernel(token, own, beyond, ons, out):
    size_x = ons.shape[1]
    own0, own1 = layers_of(own, size_x)
    out0, out1 = layers_of(out, size_x)

    def step(x, top, end):
        value0, value1 = own0[x], own1[x]
        out0[x] = row_of(ons.at[0], x) * value0 - beside(own0, x, top, end) - value1
        out1[x] = row_of(ons.at[1], x) * value1 - beside(own1, x, top, end) - (value0 + beyond[size_x + x])

    over_rows(size_x, step)


def stage_kernel(token, center, inv_half, cheb, own, beyond, mine, near, ons, ons_near, image, base, once, inner):
    image_kernel(token, own, beyond, ons, image)
    local_kernel(token, center, inv_half, cheb, mine, near, ons, ons_near, base, once, inner)


def stage(token, scalars, own, beyond, mine, near, ons, ons_near):
    _, size_x, size_y = ons.shape
    layer = pltpu.VMEM((size_x, GROUP, size_y), F32)
    chunk = struct(2 * size_x, GROUP, size_y)
    return pl.pallas_call(
        stage_kernel,
        in_specs=[SMEM] * 4 + [VMEM] * 6,
        out_specs=[VMEM] * 2,
        out_shape=[chunk, chunk],
        scratch_shapes=[layer, layer],
        compiler_params=PARAMS,
        cost_estimate=SMALL,
        name="stage",
    )(token, *scalars, own, beyond, mine, near, ons, ons_near)


def image_chunk(token, own, beyond, ons):
    return pl.pallas_call(
        image_kernel,
        in_specs=[SMEM] + [VMEM] * 3,
        out_specs=VMEM,
        out_shape=struct(*own.shape),
        compiler_params=PARAMS,
        cost_estimate=SMALL,
        name="image_chunk",
    )(token, own, beyond, ons)


def wide(refs, x, rows):
    return jnp.concatenate([jnp.concatenate([ref[x + i] for i in range(rows)], axis=1) for ref in refs], axis=0)


def products_kernel(lefts, itself, token, *refs):
    left, right, out = refs[:lefts], refs[lefts:-1], refs[-1]
    rows = left[0].shape[0]

    @pl.when(pl.program_id(0) == 0)
    def _():
        out[...] = jnp.zeros_like(out)

    here, there = wide(left, 0, rows), wide(right, 0, rows)
    if itself:
        there = jnp.concatenate([here, there], axis=0)
    out[...] += dot_wide(here, there)


def products(token, left, right, itself=False):
    rows_all, _, size_y = left[0].shape
    part = pl.BlockSpec((SPAN, GROUP, size_y), lambda b, token: (b, 0, 0))
    columns = len(right) + (len(left) if itself else 0)
    shape = (len(left) * GROUP, columns * GROUP)
    return pl.pallas_call(
        functools.partial(products_kernel, len(left), itself),
        grid_spec=pltpu.PrefetchScalarGridSpec(
            num_scalar_prefetch=1,
            grid=(rows_all // SPAN,),
            in_specs=[part] * (len(left) + len(right)),
            out_specs=pl.BlockSpec(shape, lambda b, token: (0, 0)),
        ),
        out_shape=struct(*shape),
        compiler_params=PARAMS,
        cost_estimate=SMALL,
        name="products",
    )(token, *left, *right)


def border_kernel(count, odd_ref, *refs):
    own, other, halos, next_halos, out = refs[:count], refs[count : 2 * count], refs[-5:-3], refs[-3:-1], refs[-1]
    half = own[0].shape[0]

    def step(block, total):
        x = block * SPAN

        def beyond(stacks):
            return wide([stack.at[i] for stack in stacks for i in range(stack.shape[0])], x, SPAN)

        left = jnp.concatenate([wide(other, x, SPAN), beyond(next_halos)], axis=1)
        return total + dot_wide(left, jnp.concatenate([beyond(halos), wide(own, x, SPAN)], axis=1))

    out[...] = lax.fori_loop(0, half // SPAN, step, jnp.zeros(out.shape, F32))


def own_border_kernel(count, odd_ref, *refs):
    own, halos, out = refs[:count], refs[count:-1], refs[-1]
    half = own[0].shape[0]

    def step(block, total):
        x = block * SPAN
        there = wide([stack.at[i] for stack in halos for i in range(stack.shape[0])], x, SPAN)
        return total + dot_wide(wide(own, x, SPAN), there)

    out[...] = lax.fori_loop(0, half // SPAN, step, jnp.zeros(out.shape, F32))


def border_products(odd, kernel, layers, halos):
    _, half, _, size_y = halos[0].shape
    size = sum(stack.shape[0] for stack in halos[:2]) * GROUP
    mine = pl.BlockSpec((half, GROUP, size_y), lambda b, odd: (odd[0], 0, 0))
    theirs = [pl.BlockSpec(stack.shape, lambda b, odd: (0, 0, 0, 0)) for stack in halos]
    return pl.pallas_call(
        functools.partial(kernel, size // GROUP),
        grid_spec=pltpu.PrefetchScalarGridSpec(
            num_scalar_prefetch=1,
            grid=(1,),
            in_specs=[mine] * len(layers) + theirs,
            out_specs=pl.BlockSpec((size, size), lambda b, odd: (0, 0)),
        ),
        out_shape=struct(size, size),
        compiler_params=PARAMS,
        cost_estimate=SMALL,
        name="border_products",
    )(odd, *layers, *halos)


def inverse_factor(matrix):
    size = matrix.shape[0]
    row = lax.broadcasted_iota(jnp.int32, (size, size), 0)
    col = lax.broadcasted_iota(jnp.int32, (size, size), 1)
    identity = jnp.where(row == col, 1.0, 0.0)
    work = jnp.concatenate([matrix, identity], axis=1)
    below = lax.broadcasted_iota(jnp.int32, work.shape, 0)
    for j in range(0, size, GROUP):
        columns = [jnp.broadcast_to(work[:, j + k : j + k + 1], work.shape) for k in range(GROUP)]
        rows = [work[j + k : j + k + 1, :] for k in range(GROUP)]
        steps = []
        for k in range(GROUP):
            steps.append(rows[k] / columns[k][j + k : j + k + 1, :])
            for m in range(k + 1, GROUP):
                share = columns[k][j + m : j + m + 1, :]
                rows[m] = rows[m] - share * steps[k]
                columns[m] = columns[m] - columns[k] * (share / columns[k][j + k : j + k + 1, :])
        rest = work
        for k in range(GROUP):
            rest = rest - columns[k] * steps[k]
        for k in range(GROUP):
            rest = jnp.where(below == j + k, rows[k], rest)
        work = jnp.where(below < j, work, rest)
    pivots = jnp.sum(work[:, :size] * identity, axis=1, keepdims=True)
    return work[:, size:] / jnp.sqrt(pivots)


def with_shift(gram, scale):
    row = lax.broadcasted_iota(jnp.int32, gram.shape, 0)
    col = lax.broadcasted_iota(jnp.int32, gram.shape, 1)
    return gram * scale + jnp.where(row == col, 0.25, 0.0)


def factor_kernel(scale, sums, inverse_out, projected):
    size = sums.shape[0] // 3
    own, cross, other = (sums[i * size : (i + 1) * size, :] for i in range(3))
    top = inverse_factor(with_shift(own[:, :size], scale))
    low = dot_nt(cross[:, :size] * scale, top)
    inverse = inverse_factor(with_shift(other[:, :size], scale) - dot_nt(low, low))
    side = -dot_nn(inverse, dot_nn(low, top))
    whole = jnp.concatenate(
        [jnp.concatenate([top, jnp.zeros_like(top)], axis=1), jnp.concatenate([side, inverse], axis=1)], axis=0
    )
    inverse_out[...] = whole
    here, mixed, there = own[:, size:], cross[:, size:], other[:, size:]
    upper = jnp.concatenate([here + here.T, mixed.T], axis=1)
    lower = jnp.concatenate([mixed, there + there.T], axis=1)
    matrix = jnp.concatenate([upper, lower], axis=0) * (0.5 * scale)
    projected[...] = dot_nt(dot_nn(whole, matrix), whole)


def factor(sums, scale):
    size = sums.shape[0] // 3
    return pl.pallas_call(
        functools.partial(factor_kernel, scale),
        in_specs=[VMEM],
        out_specs=[VMEM] * 2,
        out_shape=[struct(2 * size, 2 * size)] * 2,
        compiler_params=PARAMS,
        cost_estimate=SMALL,
        name="factor",
    )(sums)


def basis_kernel(count, odd_ref, *refs):
    parts, coef, out = refs[:count], refs[count], refs[-1]
    rows, _, size_y = parts[0].shape
    result = dot_tall(coef[...], wide(parts, 0, rows))
    for v in range(0, out.shape[0], GROUP):
        for j in range(0, rows, GROUP):
            pieces = [result[v : v + GROUP, (j + i) * size_y : (j + i + 1) * size_y] for i in range(GROUP)]
            out[v : v + GROUP, 0, j : j + GROUP, :] = jnp.swapaxes(jnp.stack(pieces, axis=0), 0, 1)


def basis_of(odd, parts, coef):
    rows_all, _, size_y = parts[0].shape
    layers, rows = 2, SPAN
    size_x = rows_all // layers
    blocks = size_x // rows
    size = coef.shape[0]
    part = pl.BlockSpec((rows, GROUP, size_y), lambda s, b, odd: (s * blocks + b, 0, 0))
    return pl.pallas_call(
        functools.partial(basis_kernel, len(parts)),
        grid_spec=pltpu.PrefetchScalarGridSpec(
            num_scalar_prefetch=1,
            grid=(layers, blocks),
            in_specs=[part] * len(parts) + [pl.BlockSpec(coef.shape, lambda s, b, odd: (0, 0))],
            out_specs=pl.BlockSpec((size, 1, rows, size_y), lambda s, b, odd: (0, (s + odd[0]) % 2, b, 0)),
        ),
        out_shape=struct(size, layers, size_x, size_y),
        compiler_params=PARAMS,
        cost_estimate=SMALL,
        name="basis_of",
    )(odd, *parts, coef)


def behind(value, *others):
    return lax.optimization_barrier((value, *others))[0]


def partial_sums(value, axis, *others):
    size = lax.axis_size(axis)
    if size & (size - 1):
        return [lax.psum(value, axis)]
    sums = []
    step = size // 2
    while step:
        value = value + lax.ppermute(value, axis, [(i, i ^ step) for i in range(size)])
        if not sums:
            value = behind(value, *others)
        sums.append(value)
        step //= 2
    return sums


def body(vectors, onsite, center, inv_half, cheb_coef):
    field = vectors[0]
    count, layers, size_x, size_y = field.shape
    ring = lax.axis_size("gz")
    cuts = lax.axis_size("cuts")
    scale = 1.0 / (layers * ring * size_x * size_y)
    odd = (lax.axis_index("gz") % 2).astype(jnp.int32)[None]
    across = [(i, (i + 1) % ring if i % 2 else (i - 1) % ring) for i in range(ring)]
    pair = [(i, i ^ 1) for i in range(ring)]
    left = [(i, i - 1) for i in range(1, cuts)]

    def inter_swap(value):
        return lax.ppermute(value, "gz", across)

    def intra_swap(value):
        return lax.ppermute(value, "gz", pair)

    def from_next(value):
        return lax.ppermute(value, "cuts", left)

    scalars = (center, inv_half, cheb_coef)
    ons = jnp.where(odd[0] == 0, onsite, onsite[::-1])
    groups = range(count // GROUP)

    mine, near, far = [], [], []
    token = odd
    for i in groups:
        mine.append(to_chunk(field, onsite, behind(odd, token), i))
        token = mine[-1]
    rows = layers * size_x
    near = [intra_swap(mine[0])]
    ons_near = intra_swap(ons[1])
    for i in groups[1:]:
        near.append(intra_swap(behind(mine[i], near[-1])))
    far = [inter_swap(mine[0]), inter_swap(behind(mine[1], near[0]))]

    def local(i, *tokens):
        return filter_local(behind(odd, *tokens), scalars, mine[i], near[i], ons, ons_near)

    base = local(0, mine[-1])
    far[0] = behind(far[0], base)
    ons_far = far[0][rows:].reshape(size_x, size_y)
    own, other, image, pay, beyond = [], [], [], [], []
    last = len(groups) - 1
    for i in groups:
        out, half = filter_far(behind(odd, base), scalars, base, far[i], ons, ons_far)
        own.append(out)
        pay.append(half)
        other.append(from_next(out))
        beyond.append(intra_swap(out))
        if i + 2 <= last:
            far.append(inter_swap(behind(mine[i + 2], far[i])))
        token = behind(odd, out, *other[i - 1 : i]) if i else behind(odd, out)
        if i == 0:
            base = local(1, token)
        elif i < last:
            done, base = stage(token, scalars, own[i - 1], beyond[i - 1], mine[i + 1], near[i + 1], ons, ons_near)
            image.append(done)
        else:
            image.append(image_chunk(token, own[i - 1], beyond[i - 1], ons))
            image.append(image_chunk(behind(odd, image[-1]), own[i], beyond[i], ons))

    middle = (last + 1) // 2
    halo0 = [inter_swap(behind(jnp.stack(pay[:middle]), own[-1])), inter_swap(jnp.stack(pay[middle:]))]
    both = products(odd, own, image, True)
    start = (1 - odd[0]) * (size_x // 2)
    next_pay = [lax.dynamic_slice_in_dim(behind(value, both), start, size_x // 2, 0) for value in other[:middle]]
    next_pay = inter_swap(jnp.stack(next_pay))
    border = border_products(behind(odd, both), own_border_kernel, own, halo0)
    here = jnp.concatenate([both[:, :count], both[:, count:] - 2.0 * border], axis=1)
    next_halo0 = [next_pay, from_next(behind(halo0[1], both))]
    there = from_next(here)
    cross = products(behind(odd, border), other, own + image)
    border = border_products(behind(odd, cross, there), border_kernel, own + other, halo0 + next_halo0)
    cross = jnp.concatenate([cross[:, :count], 2.0 * (cross[:, count:] - border)], axis=1)
    sums = partial_sums(jnp.concatenate([here, cross, there], axis=0), "gz")[-1]
    inverse, projected = factor(sums, scale)
    basis = basis_of(odd, own + other, inverse)
    return basis[None], projected[None]


def solution(mesh):
    in_specs = (
        P("cuts", None, "gz", None, None),
        P("gz", None, None),
        P("cuts"),
        P("cuts"),
        P("cuts", None),
    )
    out_specs = (P("cuts", None, "gz", None, None), P("cuts", None, None))
    return jax.shard_map(body, mesh=mesh, in_specs=in_specs, out_specs=out_specs, check_vma=False)
```
